32 devices in a mesh: pool: 8 (over z, core), cp: 4 (over y, x).
Axes of the slice: x: 2, y: 2, z: 4, core: 2. Of those that a mesh axis runs over, the one named last changes fastest.
Arguments:
- queries: bfloat16 [8, 512, 4096], P('pool', 'cp'), may hold values from -15 to 15
- span_keys: bfloat16 [8, 512, 512], P('pool', 'cp'), may hold values from -6 to 6
- span_values: bfloat16 [8, 512, 512], P('pool', 'cp'), may hold values from -6 to 6
- pool_keys: bfloat16 [192, 128, 512], P('pool'), may hold values from -6 to 6
- pool_values: bfloat16 [192, 128, 512], P('pool'), may hold values from -6 to 6
- page_ids: int32 [8, 16], replicated, may hold values from 0 to 191, as said below
- prefix_pages: int32 [8], replicated, may hold values from 1 to 16, as said below
Outputs:
- attended: float32 [8, 512, 4096], P('pool', 'cp')
The draws below stay inside these ranges and needn't reach their ends.
Inputs may be any that keep to these rules, and one draw needn't show every extreme that they name: `page_ids`: page p is held by index p // 24 of pool. Among the first prefix_pages[r] entries of a request, one owner holds at most 2 pages, all different; entries beyond that are unused. `prefix_pages`: some request has all 16 entries in use.
All inputs are finite; a program needn't handle non-finite values.
Results may differ from the reference program's by a relative error of at most 0.002.
Values may be sent and summed in bfloat16 or wider, within the bound.
No kernel may reach another device: no remote copies, remote signals or barrier semaphores. Data moves between devices by JAX's collectives and lax.ppermute only.
A program may use at most 128 MiB of HBM per device.

```python
import jax
import jax.numpy as jnp
from jax import lax

HEAD_DIM = 128
HEADS = 32
KV_HEADS = 4
PAGE = 128
CAP = 2
PAGES_DEV = 24
TOK_DEV = 128
SPAN = 512
REQS = 8
SLOTS = 16
POOL_PAGES = 192


def draw_queries(key, part):
    shape = (REQS, SPAN, HEADS * HEAD_DIM)
    noise_key = jax.random.fold_in(key, 5)
    return jnp.clip(2.5 * jax.random.normal(noise_key, shape, jnp.float32), -15.0, 15.0).astype(jnp.bfloat16)


def draw_span_keys(key, part):
    shape = (REQS, SPAN, KV_HEADS * HEAD_DIM)
    noise_key = jax.random.fold_in(key, 9)
    return jnp.clip(jax.random.normal(noise_key, shape, jnp.float32), -6.0, 6.0).astype(jnp.bfloat16)


def one_list(key):
    key_perm, key_base, key_off = jax.random.split(key, 3)
    owner_count = SLOTS // CAP
    band = PAGES_DEV // CAP
    perm = jax.random.permutation(key_perm, owner_count)
    slot = jnp.arange(SLOTS)
    owner = perm[slot // CAP]
    base = jax.random.randint(key_base, (owner_count,), 0, PAGES_DEV)[slot // CAP]
    offset = jax.random.randint(key_off, (SLOTS,), 0, band)
    local = (base + slot % CAP * band + offset) % PAGES_DEV
    return (owner * PAGES_DEV + local).astype(jnp.int32)


def draw_page_ids(key, part):
    keys = jax.random.split(jax.random.fold_in(key, 11), REQS)
    return jax.vmap(one_list)(keys)


def draw_prefix_pages(key, part):
    key_len, key_which = jax.random.split(jax.random.fold_in(key, 13))
    lengths = jax.random.randint(key_len, (REQS,), 1, SLOTS + 1)
    which = jax.random.randint(key_which, (), 0, REQS)
    return lengths.at[which].set(SLOTS).astype(jnp.int32)


def block_scale(stream_key, dims, shards, least, high):
    gain, own = 1.0, jax.random.fold_in(stream_key, 6)
    for position, parts in shards:
        steps = jnp.exp(jax.random.uniform(jax.random.fold_in(own, position), (parts,), jnp.float32, least / len(shards), high / len(shards)))
        gain = gain * jnp.repeat(steps, dims[position] // parts).reshape([-1 if axis == position else 1 for axis in range(len(dims))])
    return gain


def centred(stream_key, extent, deviation, most, pieces=(), kind=jnp.bfloat16):
    level = block_scale(stream_key, extent, pieces, -0.22, 0.18) if pieces else 1.0
    values = jax.random.normal(stream_key, extent, jnp.float32) * deviation * level
    return jnp.minimum(jnp.maximum(values, -most), most).astype(kind)


def setup_inputs(seed: int = 0) -> dict:
    arg_keys = jax.random.split(jax.random.key(seed), 8)
    queries = draw_queries(jax.random.fold_in(arg_keys[7], 71), 0)
    span_keys = draw_span_keys(jax.random.fold_in(arg_keys[7], 71), 0)
    span_values = centred(arg_keys[2], (REQS, SPAN, KV_HEADS * HEAD_DIM), 1.0, 6.0, ((0, 8), (1, 4)))
    pool_keys = centred(arg_keys[3], (POOL_PAGES, PAGE, KV_HEADS * HEAD_DIM), 1.0, 6.0, ((0, 8),))
    pool_values = centred(arg_keys[4], (POOL_PAGES, PAGE, KV_HEADS * HEAD_DIM), 1.0, 6.0, ((0, 8),))
    page_ids = draw_page_ids(jax.random.fold_in(arg_keys[7], 71), 0)
    prefix_pages = draw_prefix_pages(jax.random.fold_in(arg_keys[7], 71), 0)
    return dict(queries=queries, span_keys=span_keys, span_values=span_values, pool_keys=pool_keys, pool_values=pool_values, page_ids=page_ids, prefix_pages=prefix_pages)


NEG_FILL = -1e30


def one_request(inputs, pool_keys, pool_values):
    queries, span_keys, span_values, page_list, live_pages = inputs
    groups = HEADS // KV_HEADS
    width = KV_HEADS * HEAD_DIM
    prefix_keys = pool_keys[page_list].reshape(SLOTS * PAGE, width)
    prefix_values = pool_values[page_list].reshape(SLOTS * PAGE, width)
    key_row_set = jnp.concatenate([prefix_keys, span_keys], 0).astype(jnp.float32).reshape(-1, KV_HEADS, HEAD_DIM)
    value_row_set = jnp.concatenate([prefix_values, span_values], 0).astype(jnp.float32).reshape(-1, KV_HEADS, HEAD_DIM)
    slot_live = jnp.repeat(jnp.arange(SLOTS, dtype=jnp.int32) < live_pages, PAGE)
    span_pos = jnp.arange(SPAN, dtype=jnp.int32)
    score_scale = HEAD_DIM ** -0.5

    def block(index):
        begin = (index * TOK_DEV).astype(jnp.int32)
        query_block_rows = lax.dynamic_slice_in_dim(queries, begin, TOK_DEV, 0).astype(jnp.float32)
        query_block_rows = query_block_rows.reshape(TOK_DEV, KV_HEADS, groups, HEAD_DIM)
        query_pos = begin + jnp.arange(TOK_DEV, dtype=jnp.int32)
        visible = jnp.concatenate([jnp.broadcast_to(slot_live[None, :], (TOK_DEV, SLOTS * PAGE)), span_pos[None, :] <= query_pos[:, None]], 1)
        logit_scores = jnp.einsum("swxl,cwl->swxc", query_block_rows, key_row_set) * score_scale
        live = visible[:, None, None, :]
        logit_scores = jnp.where(live, logit_scores, NEG_FILL)
        peak = jnp.max(logit_scores, axis=-1, keepdims=True)
        softmax_weights = jnp.where(live, jnp.exp(logit_scores - peak), 0.0).astype(jnp.bfloat16)
        denom = jnp.sum(softmax_weights.astype(jnp.float32), axis=-1)
        weighted_values = jnp.einsum("unqy,ynx->unqx", softmax_weights.astype(jnp.float32), value_row_set)
        return (weighted_values / denom[..., None]).reshape(TOK_DEV, HEADS * HEAD_DIM)

    outputs = lax.map(block, jnp.arange(SPAN // TOK_DEV, dtype=jnp.int32))
    return outputs.reshape(SPAN, HEADS * HEAD_DIM)


def reference(queries, span_keys, span_values, pool_keys, pool_values, page_ids, prefix_pages):
    def single(inputs):
        return one_request(inputs, pool_keys, pool_values)

    return lax.map(single, (queries, span_keys, span_values, page_ids, prefix_pages))
```

```python
import functools
import math

import jax
import jax.numpy as jnp
from jax import lax
from jax.experimental import pallas as pl
from jax.experimental.pallas import tpu as pltpu
from jax.sharding import PartitionSpec as P

HEAD_DIM = 128
HEADS = 32
KV_HEADS = 4
CAP = 2

NEG_FILL = -1e30
EXP2_SCALE = math.log2(math.e) / math.sqrt(HEAD_DIM)
ANY = pl.BlockSpec(memory_space=pl.ANY)
SMEM = pl.BlockSpec(memory_space=pltpu.SMEM)
VMEM = pl.BlockSpec(memory_space=pltpu.VMEM)


def kv_head(ctx, ctx_count):
    return ctx * KV_HEADS // ctx_count


def prep_pages_kernel(ids_ref, len_ref, keys_ref, values_ref, *rest):
    pool_count = ids_ref.shape[0]
    slot_count = ids_ref.shape[1]
    out_refs = rest[:pool_count]
    pages_ref, sems = rest[pool_count:]
    pages_dev = keys_ref.shape[0]
    me = lax.axis_index("pool")
    head = kv_head(lax.axis_index("cp"), lax.axis_size("cp"))
    columns = pl.ds(pl.multiple_of(head * HEAD_DIM, HEAD_DIM), HEAD_DIM)
    low = me * pages_dev
    copies = []
    for step in reversed(range(pool_count)):
        request = me ^ step
        live = len_ref[request]
        for rank in range(CAP):
            pages_ref[step, rank] = 0
        count = jnp.int32(0)
        for slot in range(slot_count):
            local = ids_ref[request, slot] - low
            hit = (local >= 0) & (local < pages_dev) & (slot < live)
            pages_ref[step, count] = jnp.where(hit, local, 0)
            count = jnp.minimum(count + hit.astype(jnp.int32), CAP)
        for rank in range(CAP):
            page = pages_ref[step, rank]
            for which, source in enumerate((keys_ref, values_ref)):
                copy = pltpu.make_async_copy(
                    source.at[page, :, columns],
                    out_refs[step].at[which, rank],
                    sems.at[step, which, rank],
                )
                copy.start()
                copies.append(copy)
    for copy in copies:
        copy.wait()


def prep_pages(page_ids, prefix_pages, pool_keys, pool_values):
    pool_count = page_ids.shape[0]
    page = pool_keys.shape[1]
    shape = jax.ShapeDtypeStruct((2, CAP, page, HEAD_DIM), jnp.bfloat16)
    return pl.pallas_call(
        prep_pages_kernel,
        out_shape=[shape] * pool_count,
        in_specs=[SMEM, SMEM, ANY, ANY],
        out_specs=[ANY] * pool_count,
        scratch_shapes=[
            pltpu.SMEM((pool_count, CAP + 1), jnp.int32),
            pltpu.SemaphoreType.DMA((pool_count, 2, CAP)),
        ],
        name="prep_pages",
    )(page_ids, prefix_pages, pool_keys, pool_values)


def prep_span_kernel(q_ref, k_ref, v_ref, out_ref, sems):
    ctx_count = out_ref.shape[0]
    width = HEADS // ctx_count * HEAD_DIM
    copies = []
    for ctx in range(ctx_count):
        head = kv_head(ctx, ctx_count) * HEAD_DIM
        for part, (source, begin, size, place) in enumerate(
            (
                (q_ref, ctx * width, width, 0),
                (k_ref, head, HEAD_DIM, width),
                (v_ref, head, HEAD_DIM, width + HEAD_DIM),
            )
        ):
            copy = pltpu.make_async_copy(
                source.at[0, :, pl.ds(begin, size)],
                out_ref.at[ctx, :, pl.ds(place, size)],
                sems.at[ctx, part],
            )
            copy.start()
            copies.append(copy)
    for copy in copies:
        copy.wait()


def prep_span(queries, span_keys, span_values):
    ctx_count = lax.axis_size("cp")
    tok_count = queries.shape[1]
    width = (HEADS // ctx_count + 2) * HEAD_DIM
    return pl.pallas_call(
        prep_span_kernel,
        out_shape=jax.ShapeDtypeStruct((ctx_count, tok_count, width), jnp.bfloat16),
        in_specs=[ANY] * 3,
        out_specs=ANY,
        scratch_shapes=[pltpu.SemaphoreType.DMA((ctx_count, 3))],
        name="prep_span",
    )(queries, span_keys, span_values)


def attend_kernel(chunk, pages_dev, ids_ref, len_ref, span_ref, *rest):
    pool_count, slot_count = ids_ref.shape
    page_refs = rest[:pool_count]
    out_ref, k_ref, v_ref, count_ref = rest[pool_count:]
    ctx_count, tok_count, width = span_ref.shape
    heads = width // HEAD_DIM - 2
    page = page_refs[0].shape[2]
    me = lax.axis_index("pool")

    for owner in range(pool_count):
        count_ref[owner] = 0
    live = len_ref[me]
    for slot in range(slot_count):
        owner = ids_ref[me, slot] // pages_dev
        count_ref[owner] = count_ref[owner] + (slot < live).astype(jnp.int32)

    first_key = span_ref[0, 0:1, heads * HEAD_DIM : (heads + 1) * HEAD_DIM]
    first_key = jnp.broadcast_to(first_key, (page, HEAD_DIM))
    zeros = jnp.zeros((page, HEAD_DIM), jnp.bfloat16)
    ones = jnp.ones((page, HEAD_DIM), jnp.bfloat16)
    for step in range(pool_count):
        for rank in range(CAP):
            rows = pl.ds((step * CAP + rank) * page, page)
            used = count_ref[me ^ step] > rank
            k_ref[rows, :] = jnp.where(used, page_refs[step][0, rank], first_key)
            v_ref[rows, :HEAD_DIM] = jnp.where(used, page_refs[step][1, rank], zeros)
            v_ref[rows, HEAD_DIM:] = jnp.where(used, ones, zeros)
    prefix = pool_count * CAP * page
    for ctx in range(ctx_count):
        rows = pl.ds(prefix + ctx * tok_count, tok_count)
        k_ref[rows, :] = span_ref[ctx, :, heads * HEAD_DIM : (heads + 1) * HEAD_DIM]
        v_ref[rows, :HEAD_DIM] = span_ref[ctx, :, (heads + 1) * HEAD_DIM :]
        v_ref[rows, HEAD_DIM:] = ones

    row_pos = lax.broadcasted_iota(jnp.int32, (tok_count, tok_count), 0)
    col_pos = lax.broadcasted_iota(jnp.int32, (tok_count, tok_count), 1)
    causal = jnp.concatenate([col_pos <= row_pos] * heads, axis=0)

    for ctx in range(ctx_count):
        query = jnp.concatenate(
            [span_ref[ctx, :, h * HEAD_DIM : (h + 1) * HEAD_DIM] for h in range(heads)], axis=0
        )
        parts = [(begin, chunk, False) for begin in range(0, prefix, chunk)]
        if ctx:
            parts.append((prefix, ctx * tok_count, False))
        parts.append((prefix + ctx * tok_count, tok_count, True))
        scores = []
        for begin, size, diagonal in parts:
            part = lax.dot_general(
                query,
                k_ref[begin : begin + size, :],
                (((1,), (1,)), ((), ())),
                preferred_element_type=jnp.float32,
            )
            scores.append(jnp.where(causal, part, NEG_FILL) if diagonal else part)
        peak = functools.reduce(
            jnp.maximum, [jnp.max(part, axis=1, keepdims=True) for part in scores]
        )
        total = None
        for (begin, size, _), part in zip(parts, scores):
            weights = jnp.exp2((part - peak) * EXP2_SCALE).astype(jnp.bfloat16)
            term = jnp.dot(
                weights, v_ref[begin : begin + size, :], preferred_element_type=jnp.float32
            )
            total = term if total is None else total + term
        mixed = (total[:, :HEAD_DIM] / total[:, HEAD_DIM:]).astype(jnp.bfloat16)
        for h in range(heads):
            out_ref[ctx, :, h * HEAD_DIM : (h + 1) * HEAD_DIM] = mixed[
                h * tok_count : (h + 1) * tok_count
            ]


def attend(page_ids, prefix_pages, span, pages, pages_dev):
    ctx_count, tok_count, width = span.shape
    pool_count = page_ids.shape[0]
    page = pages[0].shape[2]
    prefix = pool_count * CAP * page
    rows = prefix + ctx_count * tok_count
    heads = width // HEAD_DIM - 2
    return pl.pallas_call(
        functools.partial(attend_kernel, 512, pages_dev),
        out_shape=jax.ShapeDtypeStruct((ctx_count, tok_count, heads * HEAD_DIM), jnp.bfloat16),
        in_specs=[SMEM, SMEM, VMEM] + [VMEM] * pool_count,
        out_specs=VMEM,
        scratch_shapes=[
            pltpu.VMEM((rows, HEAD_DIM), jnp.bfloat16),
            pltpu.VMEM((rows, 2 * HEAD_DIM), jnp.bfloat16),
            pltpu.SMEM((pool_count,), jnp.int32),
        ],
        compiler_params=pltpu.CompilerParams(vmem_limit_bytes=56 * 2**20),
        name="attend",
    )(page_ids, prefix_pages, span, *pages)


def body(queries, span_keys, span_values, pool_keys, pool_values, page_ids, prefix_pages):
    tok_count = queries.shape[1]
    pool_count = lax.axis_size("pool")
    pages = prep_pages(page_ids, prefix_pages, pool_keys, pool_values)
    fetched = [pages[0]]
    for step in range(1, pool_count):
        pairs = [(i, i ^ step) for i in range(pool_count)]
        fetched.append(lax.ppermute(pages[step], "pool", pairs))
    span = lax.all_to_all(
        prep_span(queries, span_keys, span_values), "cp", split_axis=0, concat_axis=0, tiled=True
    )
    mixed = attend(page_ids, prefix_pages, span, fetched, pool_keys.shape[0])
    mixed = lax.all_to_all(mixed, "cp", split_axis=0, concat_axis=0, tiled=True)
    attended = mixed.transpose(1, 0, 2).astype(jnp.float32)
    return attended.reshape(1, tok_count, HEADS * HEAD_DIM)


def solution(mesh):
    in_specs = (
        P("pool", "cp", None),
        P("pool", "cp", None),
        P("pool", "cp", None),
        P("pool", None, None),
        P("pool", None, None),
        P(),
        P(),
    )
    out_specs = P("pool", "cp", None)
    return jax.shard_map(body, mesh=mesh, in_specs=in_specs, out_specs=out_specs, check_vma=False)
```

```python
import functools
import math

import jax
import jax.numpy as jnp
from jax import lax
from jax.experimental import pallas as pl
from jax.experimental.pallas import tpu as pltpu
from jax.sharding import PartitionSpec as P

HEAD_DIM = 128
HEADS = 32
KV_HEADS = 4
CAP = 2

NEG_FILL = -1e30
EXP2_SCALE = math.log2(math.e) / math.sqrt(HEAD_DIM)
ANY = pl.BlockSpec(memory_space=pl.ANY)
SMEM = pl.BlockSpec(memory_space=pltpu.SMEM)
VMEM = pl.BlockSpec(memory_space=pltpu.VMEM)


def kv_head(ctx, ctx_count):
    return ctx * KV_HEADS // ctx_count


def prep_pages_kernel(ids_ref, len_ref, keys_ref, values_ref, *rest):
    pool_count = ids_ref.shape[0]
    slot_count = ids_ref.shape[1]
    out_refs = rest[:pool_count]
    pages_ref, sems = rest[pool_count:]
    pages_dev = keys_ref.shape[0]
    me = lax.axis_index("pool")
    head = kv_head(lax.axis_index("cp"), lax.axis_size("cp"))
    columns = pl.ds(pl.multiple_of(head * HEAD_DIM, HEAD_DIM), HEAD_DIM)
    low = me * pages_dev
    copies = []
    for step in reversed(range(pool_count)):
        request = me ^ step
        live = len_ref[request]
        for rank in range(CAP):
            pages_ref[step, rank] = 0
        count = jnp.int32(0)
        for slot in range(slot_count):
            local = ids_ref[request, slot] - low
            hit = (local >= 0) & (local < pages_dev) & (slot < live)
            pages_ref[step, count] = jnp.where(hit, local, 0)
            count = jnp.minimum(count + hit.astype(jnp.int32), CAP)
        for rank in range(CAP):
            page = pages_ref[step, rank]
            for which, source in enumerate((keys_ref, values_ref)):
                copy = pltpu.make_async_copy(
                    source.at[page, :, columns],
                    out_refs[step].at[which, rank],
                    sems.at[step, which, rank],
                )
                copy.start()
                copies.append(copy)
    for copy in copies:
        copy.wait()


def prep_pages(page_ids, prefix_pages, pool_keys, pool_values):
    pool_count = page_ids.shape[0]
    page = pool_keys.shape[1]
    shape = jax.ShapeDtypeStruct((2, CAP, page, HEAD_DIM), jnp.bfloat16)
    return pl.pallas_call(
        prep_pages_kernel,
        out_shape=[shape] * pool_count,
        in_specs=[SMEM, SMEM, ANY, ANY],
        out_specs=[VMEM] * pool_count,
        scratch_shapes=[
            pltpu.SMEM((pool_count, CAP + 1), jnp.int32),
            pltpu.SemaphoreType.DMA((pool_count, 2, CAP)),
        ],
        name="prep_pages",
    )(page_ids, prefix_pages, pool_keys, pool_values)


def prep_span_kernel(q_ref, k_ref, v_ref, _, out_ref):
    ctx_count = out_ref.shape[0]
    width = HEADS // ctx_count * HEAD_DIM
    for ctx in range(ctx_count):
        head = kv_head(ctx, ctx_count) * HEAD_DIM
        out_ref[ctx, :, :width] = q_ref[0, :, ctx * width : (ctx + 1) * width]
        out_ref[ctx, :, width : width + HEAD_DIM] = k_ref[0, :, head : head + HEAD_DIM]
        out_ref[ctx, :, width + HEAD_DIM :] = v_ref[0, :, head : head + HEAD_DIM]


def prep_span(queries, span_keys, span_values, after):
    ctx_count = lax.axis_size("cp")
    tok_count = queries.shape[1]
    width = (HEADS // ctx_count + 2) * HEAD_DIM
    return pl.pallas_call(
        prep_span_kernel,
        out_shape=jax.ShapeDtypeStruct((ctx_count, tok_count, width), jnp.bfloat16),
        in_specs=[VMEM] * 3 + [ANY],
        out_specs=VMEM,
        name="prep_span",
    )(queries, span_keys, span_values, after)


def widen_kernel(in_ref, out_ref):
    out_ref[0] = in_ref[0].astype(jnp.float32)


def widen(mixed):
    count, tok_count, width = mixed.shape
    return pl.pallas_call(
        widen_kernel,
        grid=(count,),
        out_shape=jax.ShapeDtypeStruct((1, tok_count, count * width), jnp.float32),
        in_specs=[pl.BlockSpec((1, tok_count, width), lambda i: (i, 0, 0))],
        out_specs=pl.BlockSpec((1, tok_count, width), lambda i: (0, 0, i)),
        name="widen",
    )(mixed)


def attend_kernel(chunk, pages_dev, ids_ref, len_ref, span_ref, *rest):
    pool_count, slot_count = ids_ref.shape
    page_refs = rest[:pool_count]
    out_ref, k_ref, v_ref, count_ref = rest[pool_count:]
    ctx_count, tok_count, width = span_ref.shape
    heads = width // HEAD_DIM - 2
    page = page_refs[0].shape[2]
    me = lax.axis_index("pool")

    for owner in range(pool_count):
        count_ref[owner] = 0
    live = len_ref[me]
    for slot in range(slot_count):
        owner = ids_ref[me, slot] // pages_dev
        count_ref[owner] = count_ref[owner] + (slot < live).astype(jnp.int32)

    first_key = span_ref[0, 0:1, heads * HEAD_DIM : (heads + 1) * HEAD_DIM]
    first_key = jnp.broadcast_to(first_key, (page, HEAD_DIM))
    zeros = jnp.zeros((page, HEAD_DIM), jnp.bfloat16)
    ones = jnp.ones((page, HEAD_DIM), jnp.bfloat16)
    for step in range(pool_count):
        for rank in range(CAP):
            rows = pl.ds((step * CAP + rank) * page, page)
            used = count_ref[me ^ step] > rank
            k_ref[rows, :] = jnp.where(used, page_refs[step][0, rank], first_key)
            v_ref[rows, :HEAD_DIM] = jnp.where(used, page_refs[step][1, rank], zeros)
            v_ref[rows, HEAD_DIM:] = jnp.where(used, ones, zeros)
    prefix = pool_count * CAP * page
    for ctx in range(ctx_count):
        rows = pl.ds(prefix + ctx * tok_count, tok_count)
        k_ref[rows, :] = span_ref[ctx, :, heads * HEAD_DIM : (heads + 1) * HEAD_DIM]
        v_ref[rows, :HEAD_DIM] = span_ref[ctx, :, (heads + 1) * HEAD_DIM :]
        v_ref[rows, HEAD_DIM:] = ones

    row_pos = lax.broadcasted_iota(jnp.int32, (tok_count, tok_count), 0)
    col_pos = lax.broadcasted_iota(jnp.int32, (tok_count, tok_count), 1)
    causal = jnp.concatenate([col_pos <= row_pos] * heads, axis=0)

    for ctx in range(ctx_count):
        query = jnp.concatenate(
            [span_ref[ctx, :, h * HEAD_DIM : (h + 1) * HEAD_DIM] for h in range(heads)], axis=0
        )
        parts = [(begin, chunk, False) for begin in range(0, prefix, chunk)]
        if ctx:
            parts.append((prefix, ctx * tok_count, False))
        parts.append((prefix + ctx * tok_count, tok_count, True))
        scores = []
        for begin, size, diagonal in parts:
            part = lax.dot_general(
                query,
                k_ref[begin : begin + size, :],
                (((1,), (1,)), ((), ())),
                preferred_element_type=jnp.float32,
            )
            scores.append(jnp.where(causal, part, NEG_FILL) if diagonal else part)
        peak = functools.reduce(
            jnp.maximum, [jnp.max(part, axis=1, keepdims=True) for part in scores]
        )
        total = None
        for (begin, size, _), part in zip(parts, scores):
            weights = jnp.exp2((part - peak) * EXP2_SCALE).astype(jnp.bfloat16)
            term = jnp.dot(
                weights, v_ref[begin : begin + size, :], preferred_element_type=jnp.float32
            )
            total = term if total is None else total + term
        mixed = (total[:, :HEAD_DIM] / total[:, HEAD_DIM:]).astype(jnp.bfloat16)
        for h in range(heads):
            out_ref[ctx, :, h * HEAD_DIM : (h + 1) * HEAD_DIM] = mixed[
                h * tok_count : (h + 1) * tok_count
            ]


def attend(page_ids, prefix_pages, span, pages, pages_dev):
    ctx_count, tok_count, width = span.shape
    pool_count = page_ids.shape[0]
    page = pages[0].shape[2]
    prefix = pool_count * CAP * page
    rows = prefix + ctx_count * tok_count
    heads = width // HEAD_DIM - 2
    return pl.pallas_call(
        functools.partial(attend_kernel, 512, pages_dev),
        out_shape=jax.ShapeDtypeStruct((ctx_count, tok_count, heads * HEAD_DIM), jnp.bfloat16),
        in_specs=[SMEM, SMEM, VMEM] + [VMEM] * pool_count,
        out_specs=VMEM,
        scratch_shapes=[
            pltpu.VMEM((rows, HEAD_DIM), jnp.bfloat16),
            pltpu.VMEM((rows, 2 * HEAD_DIM), jnp.bfloat16),
            pltpu.SMEM((pool_count,), jnp.int32),
        ],
        compiler_params=pltpu.CompilerParams(vmem_limit_bytes=56 * 2**20),
        name="attend",
    )(page_ids, prefix_pages, span, *pages)


def body(queries, span_keys, span_values, pool_keys, pool_values, page_ids, prefix_pages):
    pool_count = lax.axis_size("pool")
    pages = prep_pages(page_ids, prefix_pages, pool_keys, pool_values)
    fetched = [pages[0]]
    for step in range(1, pool_count):
        pairs = [(i, i ^ step) for i in range(pool_count)]
        fetched.append(lax.ppermute(pages[step], "pool", pairs))
    span = lax.all_to_all(
        prep_span(queries, span_keys, span_values, pages[0]), "cp", split_axis=0, concat_axis=0, tiled=True
    )
    mixed = attend(page_ids, prefix_pages, span, fetched, pool_keys.shape[0])
    mixed = lax.all_to_all(mixed, "cp", split_axis=0, concat_axis=0, tiled=True)
    return widen(mixed)


def solution(mesh):
    in_specs = (
        P("pool", "cp", None),
        P("pool", "cp", None),
        P("pool", "cp", None),
        P("pool", None, None),
        P("pool", None, None),
        P(),
        P(),
    )
    out_specs = P("pool", "cp", None)
    return jax.shard_map(body, mesh=mesh, in_specs=in_specs, out_specs=out_specs, check_vma=False)
```

```python
import functools
import math

import jax
import jax.numpy as jnp
from jax import lax
from jax.experimental import pallas as pl
from jax.experimental.pallas import tpu as pltpu
from jax.sharding import PartitionSpec as P

HEAD_DIM = 128
HEADS = 32
KV_HEADS = 4
CAP = 2

NEG_FILL = -1e30
EXP2_SCALE = math.log2(math.e) / math.sqrt(HEAD_DIM)
SMALL = 8 * 2**20
ANY = pl.BlockSpec(memory_space=pl.ANY)
HBM = pl.BlockSpec(memory_space=pltpu.HBM)
SMEM = pl.BlockSpec(memory_space=pltpu.SMEM)
VMEM = pl.BlockSpec(memory_space=pltpu.VMEM)


def kv_head(ctx, ctx_count):
    return ctx * KV_HEADS // ctx_count


def pack_kernel(ids_ref, len_ref, q_ref, k_ref, v_ref, keys_ref, values_ref, *rest):
    pool_count, slot_count = ids_ref.shape
    span_ref, page_refs = rest[0], rest[1 : 1 + pool_count]
    found_ref, span_sems, sems = rest[1 + pool_count :]
    ctx_count = span_ref.shape[0]
    pages_dev = keys_ref.shape[0]
    me = lax.axis_index("pool")
    width = HEADS // ctx_count * HEAD_DIM
    copies = []
    for ctx in range(ctx_count):
        head = kv_head(ctx, ctx_count) * HEAD_DIM
        for part, (source, begin, size, place) in enumerate(
            (
                (q_ref, ctx * width, width, 0),
                (k_ref, head, HEAD_DIM, width),
                (v_ref, head, HEAD_DIM, width + HEAD_DIM),
            )
        ):
            copy = pltpu.make_async_copy(
                source.at[0, :, pl.ds(begin, size)],
                span_ref.at[ctx, :, pl.ds(place, size)],
                span_sems.at[ctx, part],
            )
            copy.start()
            copies.append(copy)
    head = kv_head(lax.axis_index("cp"), ctx_count)
    columns = pl.ds(pl.multiple_of(head * HEAD_DIM, HEAD_DIM), HEAD_DIM)
    low = me * pages_dev
    for step in reversed(range(pool_count)):
        request = me ^ step
        live = len_ref[request]
        for rank in range(CAP):
            found_ref[step, rank] = 0
        count = jnp.int32(0)
        for slot in range(slot_count):
            local = ids_ref[request, slot] - low
            hit = (local >= 0) & (local < pages_dev) & (slot < live)
            found_ref[step, count] = jnp.where(hit, local, 0)
            count = jnp.minimum(count + hit.astype(jnp.int32), CAP)
        for rank in range(CAP):
            page = found_ref[step, rank]
            for which, source in enumerate((keys_ref, values_ref)):
                copy = pltpu.make_async_copy(
                    source.at[page, :, columns],
                    page_refs[step].at[which, rank],
                    sems.at[step, which, rank],
                )
                copy.start()
                copies.append(copy)
    for copy in copies:
        copy.wait()


def pack(page_ids, prefix_pages, queries, span_keys, span_values, pool_keys, pool_values):
    ctx_count = lax.axis_size("cp")
    tok_count = queries.shape[1]
    width = (HEADS // ctx_count + 2) * HEAD_DIM
    pool_count = page_ids.shape[0]
    page = pool_keys.shape[1]
    shape = jax.ShapeDtypeStruct((2, CAP, page, HEAD_DIM), jnp.bfloat16)
    span, *pages = pl.pallas_call(
        pack_kernel,
        out_shape=[jax.ShapeDtypeStruct((ctx_count, tok_count, width), jnp.bfloat16)]
        + [shape] * pool_count,
        in_specs=[SMEM, SMEM] + [HBM] * 5,
        out_specs=[VMEM] * (1 + pool_count),
        scratch_shapes=[
            pltpu.SMEM((pool_count, CAP + 1), jnp.int32),
            pltpu.SemaphoreType.DMA((ctx_count, 3)),
            pltpu.SemaphoreType.DMA((pool_count, 2, CAP)),
        ],
        compiler_params=pltpu.CompilerParams(vmem_limit_bytes=59 * 2**20),
        name="pack",
    )(page_ids, prefix_pages, queries, span_keys, span_values, pool_keys, pool_values)
    return span, pages


def count_pages(ids_ref, len_ref, count_ref, pages_dev):
    me = lax.axis_index("pool")
    for owner in range(ids_ref.shape[0]):
        count_ref[owner] = 0
    live = len_ref[me]
    for slot in range(ids_ref.shape[1]):
        owner = ids_ref[me, slot] // pages_dev
        count_ref[owner] = count_ref[owner] + (slot < live).astype(jnp.int32)


def place_pages(steps, count_ref, span_ref, page_refs, k_ref, v_ref):
    me = lax.axis_index("pool")
    page = page_refs[0].shape[2]
    begin = span_ref.shape[2] - 2 * HEAD_DIM
    first_key = jnp.broadcast_to(span_ref[0, 0:1, begin : begin + HEAD_DIM], (page, HEAD_DIM))
    zeros = jnp.zeros((page, HEAD_DIM), jnp.bfloat16)
    ones = jnp.ones((page, HEAD_DIM), jnp.bfloat16)
    row = 0
    for step, page_ref in zip(steps, page_refs):
        for rank in range(CAP):
            rows = pl.ds(row, page)
            used = count_ref[me ^ step] > rank
            k_ref[rows, :] = jnp.where(used, page_ref[0, rank], first_key)
            v_ref[rows, :HEAD_DIM] = jnp.where(used, page_ref[1, rank], zeros)
            v_ref[rows, HEAD_DIM:] = jnp.where(used, ones, zeros)
            row += page


def stack_heads(span_ref, ctx, first, count):
    return jnp.concatenate(
        [
            span_ref[ctx, :, h * HEAD_DIM : (h + 1) * HEAD_DIM]
            for h in range(first, first + count)
        ],
        axis=0,
    )


def score(query, keys):
    return lax.dot_general(
        query, keys, (((1,), (1,)), ((), ())), preferred_element_type=jnp.float32
    )


def weigh(part, peak, values):
    weights = jnp.exp2((part - peak) * EXP2_SCALE).astype(jnp.bfloat16)
    return jnp.dot(weights, values, preferred_element_type=jnp.float32)


def near_kernel(chunk, pages_dev, steps, ids_ref, len_ref, span_ref, *rest):
    page_refs = rest[: len(steps)]
    sum_ref, peak_ref, k_ref, v_ref, count_ref = rest[len(steps) :]
    ctx_count, tok_count, width = span_ref.shape
    heads = width // HEAD_DIM - 2
    count_pages(ids_ref, len_ref, count_ref, pages_dev)
    place_pages(steps, count_ref, span_ref, page_refs, k_ref, v_ref)
    prefix = k_ref.shape[0] - ctx_count * tok_count
    for ctx in range(ctx_count):
        rows = pl.ds(prefix + ctx * tok_count, tok_count)
        k_ref[rows, :] = span_ref[ctx, :, heads * HEAD_DIM : (heads + 1) * HEAD_DIM]
        v_ref[rows, :HEAD_DIM] = span_ref[ctx, :, (heads + 1) * HEAD_DIM :]
        v_ref[rows, HEAD_DIM:] = jnp.ones((tok_count, HEAD_DIM), jnp.bfloat16)

    row_pos = lax.broadcasted_iota(jnp.int32, (tok_count, tok_count), 0)
    col_pos = lax.broadcasted_iota(jnp.int32, (tok_count, tok_count), 1)
    group = 256 // tok_count
    causal = jnp.concatenate([col_pos <= row_pos] * group, axis=0)
    for ctx in range(ctx_count):
        parts = [(begin, chunk, False) for begin in range(0, prefix, chunk)]
        if ctx:
            parts.append((prefix, ctx * tok_count, False))
        parts.append((prefix + ctx * tok_count, tok_count, True))
        for first in range(0, heads, group):
            rows = pl.ds(first * tok_count, group * tok_count)
            query = stack_heads(span_ref, ctx, first, group)
            scores = []
            for begin, size, diagonal in parts:
                part = score(query, k_ref[begin : begin + size, :])
                scores.append(jnp.where(causal, part, NEG_FILL) if diagonal else part)
            peak = functools.reduce(
                jnp.maximum, [jnp.max(part, axis=1, keepdims=True) for part in scores]
            )
            total = None
            for (begin, size, _), part in zip(parts, scores):
                term = weigh(part, peak, v_ref[begin : begin + size, :])
                total = term if total is None else total + term
            sum_ref[ctx, rows, :] = total
            peak_ref[ctx, rows, :] = jnp.broadcast_to(peak, (group * tok_count, HEAD_DIM))


def attend_near(page_ids, prefix_pages, span, pages, steps, pages_dev):
    ctx_count, tok_count, width = span.shape
    pool_count = page_ids.shape[0]
    page = pages[0].shape[2]
    keys = len(steps) * CAP * page + ctx_count * tok_count
    rows = (width // HEAD_DIM - 2) * tok_count
    return pl.pallas_call(
        functools.partial(near_kernel, 512, pages_dev, steps),
        out_shape=[
            jax.ShapeDtypeStruct((ctx_count, rows, 2 * HEAD_DIM), jnp.float32),
            jax.ShapeDtypeStruct((ctx_count, rows, HEAD_DIM), jnp.float32),
        ],
        in_specs=[SMEM, SMEM, VMEM] + [VMEM] * len(steps),
        out_specs=[VMEM, VMEM],
        scratch_shapes=[
            pltpu.VMEM((keys, HEAD_DIM), jnp.bfloat16),
            pltpu.VMEM((keys, 2 * HEAD_DIM), jnp.bfloat16),
            pltpu.SMEM((pool_count,), jnp.int32),
        ],
        compiler_params=pltpu.CompilerParams(vmem_limit_bytes=40 * 2**20),
        name="attend_near",
    )(page_ids, prefix_pages, span, *pages)


def far_kernel(chunk, pages_dev, steps, ctx_step, ids_ref, len_ref, span_ref, sum_ref, peak_ref, *rest):
    page_refs = rest[: len(steps)]
    out_ref, k_ref, v_ref, count_ref = rest[len(steps) :]
    tok_count = span_ref.shape[1]
    ctx = lax.axis_index("cp") ^ ctx_step
    count_pages(ids_ref, len_ref, count_ref, pages_dev)
    place_pages(steps, count_ref, span_ref, page_refs, k_ref, v_ref)
    keys = k_ref.shape[0]
    begins = range(0, keys, chunk)
    group = 256 // tok_count
    for first in range(0, span_ref.shape[2] // HEAD_DIM - 2, group):
        rows = pl.ds(first * tok_count, group * tok_count)
        query = stack_heads(span_ref, ctx, first, group)
        scores = [score(query, k_ref[begin : begin + chunk, :]) for begin in begins]
        near_peak = peak_ref[ctx, rows, :1]
        peak = functools.reduce(
            jnp.maximum, [jnp.max(part, axis=1, keepdims=True) for part in scores], near_peak
        )
        total = sum_ref[ctx, rows, :] * jnp.exp2((near_peak - peak) * EXP2_SCALE)
        for begin, part in zip(begins, scores):
            total = total + weigh(part, peak, v_ref[begin : begin + chunk, :])
        mixed = (total[:, :HEAD_DIM] / total[:, HEAD_DIM:]).astype(out_ref.dtype)
        for h in range(group):
            place = (first + h) * HEAD_DIM
            out_ref[:, place : place + HEAD_DIM] = mixed[h * tok_count : (h + 1) * tok_count]


def attend_far(page_ids, prefix_pages, span, state, pages, steps, pages_dev, ctx_step):
    ctx_count, tok_count, width = span.shape
    pool_count = page_ids.shape[0]
    page = pages[0].shape[2]
    keys = len(steps) * CAP * page
    kind = jnp.bfloat16 if ctx_step else jnp.float32
    return pl.pallas_call(
        functools.partial(far_kernel, 512, pages_dev, steps, ctx_step),
        out_shape=jax.ShapeDtypeStruct((tok_count, width - 2 * HEAD_DIM), kind),
        in_specs=[SMEM, SMEM, VMEM, VMEM, VMEM] + [VMEM] * len(steps),
        out_specs=VMEM,
        scratch_shapes=[
            pltpu.VMEM((keys, HEAD_DIM), jnp.bfloat16),
            pltpu.VMEM((keys, 2 * HEAD_DIM), jnp.bfloat16),
            pltpu.SMEM((pool_count,), jnp.int32),
        ],
        compiler_params=pltpu.CompilerParams(vmem_limit_bytes=40 * 2**20),
        name="attend_far",
    )(page_ids, prefix_pages, span, *state, *pages)


def join_kernel(*refs):
    count = len(refs) - 3
    part_refs, (out_ref, wide_ref, sems) = refs[:count], refs[count:]
    me = lax.axis_index("cp")
    width = part_refs[0].shape[1]
    copies = []
    for step, part_ref in enumerate(part_refs):
        source = part_ref
        if step:
            source = wide_ref.at[step - 1]
            source[...] = part_ref[...].astype(jnp.float32)
        place = pl.ds(pl.multiple_of((me ^ step) * width, width), width)
        copy = pltpu.make_async_copy(source, out_ref.at[0, :, place], sems.at[step])
        copy.start()
        copies.append(copy)
    for copy in copies:
        copy.wait()


def join(parts):
    tok_count, width = parts[0].shape
    count = len(parts)
    return pl.pallas_call(
        join_kernel,
        out_shape=jax.ShapeDtypeStruct((1, tok_count, count * width), jnp.float32),
        in_specs=[VMEM] * count,
        out_specs=ANY,
        scratch_shapes=[
            pltpu.VMEM((count - 1, tok_count, width), jnp.float32),
            pltpu.SemaphoreType.DMA((count,)),
        ],
        compiler_params=pltpu.CompilerParams(vmem_limit_bytes=SMALL),
        name="join",
    )(*parts)


def swap(x, axis, step):
    return lax.ppermute(x, axis, [(i, i ^ step) for i in range(lax.axis_size(axis))])


def body(queries, span_keys, span_values, pool_keys, pool_values, page_ids, prefix_pages):
    pool_count = lax.axis_size("pool")
    ctx_count = lax.axis_size("cp")
    pages_dev = pool_keys.shape[0]
    packed, pages = pack(
        page_ids, prefix_pages, queries, span_keys, span_values, pool_keys, pool_values
    )
    fetched = [pages[0]] + [swap(pages[step], "pool", step) for step in range(1, pool_count)]
    span = lax.all_to_all(packed, "cp", split_axis=0, concat_axis=0, tiled=True)
    near = tuple(range(pool_count // 2))
    far = tuple(range(pool_count // 2, pool_count))
    state = attend_near(page_ids, prefix_pages, span, fetched[: len(near)], near, pages_dev)
    parts = [None] * ctx_count
    for step in list(range(ctx_count - 1, -1, -1)):
        part = attend_far(
            page_ids, prefix_pages, span, state, fetched[len(near) :], far, pages_dev, step
        )
        parts[step] = swap(part, "cp", step) if step else part
    return join(parts)


def solution(mesh):
    in_specs = (
        P("pool", "cp", None),
        P("pool", "cp", None),
        P("pool", "cp", None),
        P("pool", None, None),
        P("pool", None, None),
        P(),
        P(),
    )
    out_specs = P("pool", "cp", None)
    return jax.shard_map(body, mesh=mesh, in_specs=in_specs, out_specs=out_specs, check_vma=False)
```

```python
import functools
import math

import jax
import jax.numpy as jnp
from jax import lax
from jax.experimental import pallas as pl
from jax.experimental.pallas import tpu as pltpu
from jax.sharding import PartitionSpec as P

HEAD_DIM = 128
HEADS = 32
KV_HEADS = 4
CAP = 2

NEG_FILL = -1e30
EXP2_SCALE = math.log2(math.e) / math.sqrt(HEAD_DIM)
SMALL = 8 * 2**20
KERNEL_VMEM = 32 * 2**20
ROWS = 256
ANY = pl.BlockSpec(memory_space=pl.ANY)
HBM = pl.BlockSpec(memory_space=pltpu.HBM)
SMEM = pl.BlockSpec(memory_space=pltpu.SMEM)
VMEM = pl.BlockSpec(memory_space=pltpu.VMEM)


def kv_head(ctx, ctx_count):
    return ctx * KV_HEADS // ctx_count


def pack_kernel(ids_hbm, len_hbm, q_ref, k_ref, v_ref, keys_ref, values_ref, *rest):
    span_out, rest = rest[0], rest[1:]
    pool_count, slot_count = ids_hbm.shape
    page_outs, rest = rest[:pool_count], rest[pool_count:]
    used_ref, ids_ref, len_ref, found_ref, span_ref, pages_ref, list_sems, span_sems, sems, out_sems = rest
    ctx_count = span_ref.shape[0]
    pages_dev = keys_ref.shape[0]
    me = lax.axis_index("pool")
    lists = [
        pltpu.make_async_copy(ids_hbm, ids_ref, list_sems.at[0]),
        pltpu.make_async_copy(len_hbm, len_ref, list_sems.at[1]),
    ]
    for copy in lists:
        copy.start()
    width = HEADS // ctx_count * HEAD_DIM
    span_copies = []
    for ctx in range(ctx_count):
        head = kv_head(ctx, ctx_count) * HEAD_DIM
        for part, (source, begin, size, place) in enumerate(
            (
                (q_ref, ctx * width, width, 0),
                (k_ref, head, HEAD_DIM, width),
                (v_ref, head, HEAD_DIM, width + HEAD_DIM),
            )
        ):
            copy = pltpu.make_async_copy(
                source.at[0, :, pl.ds(begin, size)],
                span_ref.at[ctx, :, pl.ds(place, size)],
                span_sems.at[ctx, part],
            )
            copy.start()
            span_copies.append(copy)
    for copy in lists:
        copy.wait()
    head = kv_head(lax.axis_index("cp"), ctx_count)
    columns = pl.ds(pl.multiple_of(head * HEAD_DIM, HEAD_DIM), HEAD_DIM)
    low = me * pages_dev
    page_copies = []
    for step in reversed(range(pool_count)):
        request = me ^ step
        live = len_ref[request]
        for rank in range(CAP):
            found_ref[step, rank] = 0
        count = jnp.int32(0)
        for slot in range(slot_count):
            local = ids_ref[request, slot] - low
            hit = (local >= 0) & (local < pages_dev) & (slot < live)
            found_ref[step, count] = jnp.where(hit, local, 0)
            count = jnp.minimum(count + hit.astype(jnp.int32), CAP)
        for rank in range(CAP):
            page = found_ref[step, rank]
            for which, source in enumerate((keys_ref, values_ref)):
                copy = pltpu.make_async_copy(
                    source.at[page, :, columns],
                    pages_ref.at[step, which, rank],
                    sems.at[step, which, rank],
                )
                copy.start()
                page_copies.append(copy)
    out_copies = [pltpu.make_async_copy(span_ref, span_out, out_sems.at[pool_count])]
    for copy in span_copies:
        copy.wait()
    out_copies[0].start()
    live = len_ref[me]
    for step in range(pool_count):
        count = jnp.int32(0)
        low = (me ^ step) * pages_dev
        for slot in range(slot_count):
            local = ids_ref[me, slot] - low
            hit = (local >= 0) & (local < pages_dev) & (slot < live)
            count = count + hit.astype(jnp.int32)
        for rank in range(CAP):
            row = step * CAP + rank
            used_ref[row : row + 1, :] = jnp.full(
                (1, HEAD_DIM), jnp.where(count > rank, 1.0, 0.0), jnp.float32
            )
    for index, step in enumerate(reversed(range(pool_count))):
        for copy in page_copies[index * 2 * CAP : (index + 1) * 2 * CAP]:
            copy.wait()
        copy = pltpu.make_async_copy(pages_ref.at[step], page_outs[step], out_sems.at[step])
        copy.start()
        out_copies.append(copy)
    for copy in out_copies:
        copy.wait()


def pack(page_ids, prefix_pages, queries, span_keys, span_values, pool_keys, pool_values):
    ctx_count = lax.axis_size("cp")
    tok_count = queries.shape[1]
    width = (HEADS // ctx_count + 2) * HEAD_DIM
    pool_count = page_ids.shape[0]
    page = pool_keys.shape[1]
    span_shape = (ctx_count, tok_count, width)
    page_shape = (2, CAP, page, HEAD_DIM)
    span, *pages, used = pl.pallas_call(
        pack_kernel,
        out_shape=[jax.ShapeDtypeStruct(span_shape, jnp.bfloat16)]
        + [jax.ShapeDtypeStruct(page_shape, jnp.bfloat16)] * pool_count
        + [jax.ShapeDtypeStruct((pool_count * CAP, HEAD_DIM), jnp.float32)],
        in_specs=[HBM] * 7,
        out_specs=[HBM] * (1 + pool_count) + [VMEM],
        scratch_shapes=[
            pltpu.SMEM(page_ids.shape, jnp.int32),
            pltpu.SMEM(prefix_pages.shape, jnp.int32),
            pltpu.SMEM((pool_count, CAP + 1), jnp.int32),
            pltpu.VMEM(span_shape, jnp.bfloat16),
            pltpu.VMEM((pool_count,) + page_shape, jnp.bfloat16),
            pltpu.SemaphoreType.DMA((2,)),
            pltpu.SemaphoreType.DMA((ctx_count, 3)),
            pltpu.SemaphoreType.DMA((pool_count, 2, CAP)),
            pltpu.SemaphoreType.DMA((pool_count + 1,)),
        ],
        compiler_params=pltpu.CompilerParams(vmem_limit_bytes=59 * 2**20),
        name="pack",
    )(page_ids, prefix_pages, queries, span_keys, span_values, pool_keys, pool_values)
    return span, pages, used


def place_pages(steps, used_ref, page_refs, k_ref, v_ref):
    page = page_refs[0].shape[2]
    ones = jnp.ones((page, HEAD_DIM), jnp.bfloat16)
    biases = []
    row = 0
    for step, page_ref in zip(steps, page_refs):
        for rank in range(CAP):
            rows = pl.ds(row, page)
            used = used_ref[step * CAP + rank : step * CAP + rank + 1, :]
            kept = jnp.broadcast_to(used, (page, HEAD_DIM)).astype(jnp.bfloat16)
            k_ref[rows, :] = page_ref[0, rank]
            v_ref[rows, :HEAD_DIM] = page_ref[1, rank] * kept
            v_ref[rows, HEAD_DIM:] = ones * kept
            biases.append((1.0 - used) * NEG_FILL)
            row += page
    return jnp.concatenate(biases, axis=1)


def stack_heads(span_ref, ctx, first, count):
    return jnp.concatenate(
        [
            span_ref[ctx, :, h * HEAD_DIM : (h + 1) * HEAD_DIM]
            for h in range(first, first + count)
        ],
        axis=0,
    )


def score(query, keys):
    return lax.dot_general(
        query, keys, (((1,), (1,)), ((), ())), preferred_element_type=jnp.float32
    )


def weigh(part, peak, values):
    weights = jnp.exp2((part - peak) * EXP2_SCALE).astype(jnp.bfloat16)
    return jnp.dot(weights, values, preferred_element_type=jnp.float32)


def near_kernel(steps, used_ref, span_ref, *rest):
    page_refs = rest[: len(steps)]
    sum_ref, peak_ref, k_ref, v_ref = rest[len(steps) :]
    ctx_count, tok_count, width = span_ref.shape
    heads = width // HEAD_DIM - 2
    bias = place_pages(steps, used_ref, page_refs, k_ref, v_ref)
    prefix = k_ref.shape[0] - ctx_count * tok_count
    for ctx in range(ctx_count):
        rows = pl.ds(prefix + ctx * tok_count, tok_count)
        k_ref[rows, :] = span_ref[ctx, :, heads * HEAD_DIM : (heads + 1) * HEAD_DIM]
        v_ref[rows, :HEAD_DIM] = span_ref[ctx, :, (heads + 1) * HEAD_DIM :]
        v_ref[rows, HEAD_DIM:] = jnp.ones((tok_count, HEAD_DIM), jnp.bfloat16)

    row_pos = lax.broadcasted_iota(jnp.int32, (tok_count, tok_count), 0)
    col_pos = lax.broadcasted_iota(jnp.int32, (tok_count, tok_count), 1)
    group = ROWS // tok_count
    causal = jnp.concatenate([col_pos <= row_pos] * group, axis=0)
    for ctx in range(ctx_count):
        begin = prefix + ctx * tok_count
        end = begin + tok_count
        for first in range(0, heads, group):
            rows = pl.ds(first * tok_count, group * tok_count)
            part = score(stack_heads(span_ref, ctx, first, group), k_ref[:end, :])
            pieces = [part[:, :prefix] + bias]
            if ctx:
                pieces.append(part[:, prefix:begin])
            pieces.append(jnp.where(causal, part[:, begin:], NEG_FILL))
            part = jnp.concatenate(pieces, axis=1)
            peak = jnp.max(part, axis=1, keepdims=True)
            sum_ref[ctx, rows, :] = weigh(part, peak, v_ref[:end, :])
            peak_ref[ctx, rows, :] = jnp.broadcast_to(peak, (group * tok_count, HEAD_DIM))


def attend_near(used, span, pages, steps):
    ctx_count, tok_count, width = span.shape
    page = pages[0].shape[2]
    keys = len(steps) * CAP * page + ctx_count * tok_count
    rows = (width // HEAD_DIM - 2) * tok_count
    return pl.pallas_call(
        functools.partial(near_kernel, steps),
        out_shape=[
            jax.ShapeDtypeStruct((ctx_count, rows, 2 * HEAD_DIM), jnp.float32),
            jax.ShapeDtypeStruct((ctx_count, rows, HEAD_DIM), jnp.float32),
        ],
        in_specs=[VMEM] * (2 + len(steps)),
        out_specs=[VMEM, VMEM],
        scratch_shapes=[
            pltpu.VMEM((keys, HEAD_DIM), jnp.bfloat16),
            pltpu.VMEM((keys, 2 * HEAD_DIM), jnp.bfloat16),
        ],
        compiler_params=pltpu.CompilerParams(vmem_limit_bytes=KERNEL_VMEM),
        name="attend_near",
    )(used, span, *pages)


def far_kernel(steps, ctx_step, used_ref, span_ref, sum_ref, peak_ref, *rest):
    page_refs = rest[: len(steps)]
    out_ref, k_ref, v_ref = rest[len(steps) :]
    tok_count = span_ref.shape[1]
    ctx = lax.axis_index("cp") ^ ctx_step
    bias = place_pages(steps, used_ref, page_refs, k_ref, v_ref)
    group = ROWS // tok_count
    for first in range(0, span_ref.shape[2] // HEAD_DIM - 2, group):
        rows = pl.ds(first * tok_count, group * tok_count)
        part = score(stack_heads(span_ref, ctx, first, group), k_ref[...]) + bias
        near_peak = peak_ref[ctx, rows, :1]
        peak = jnp.maximum(jnp.max(part, axis=1, keepdims=True), near_peak)
        total = weigh(part, peak, v_ref[...])
        total = total + sum_ref[ctx, rows, :] * jnp.exp2((near_peak - peak) * EXP2_SCALE)
        mixed = (total[:, :HEAD_DIM] / total[:, HEAD_DIM:]).astype(out_ref.dtype)
        for h in range(group):
            place = (first + h) * HEAD_DIM
            out_ref[:, place : place + HEAD_DIM] = mixed[h * tok_count : (h + 1) * tok_count]


def attend_far(used, span, state, pages, steps, ctx_step):
    ctx_count, tok_count, width = span.shape
    keys = len(steps) * CAP * pages[0].shape[2]
    kind = jnp.bfloat16 if ctx_step else jnp.float32
    return pl.pallas_call(
        functools.partial(far_kernel, steps, ctx_step),
        out_shape=jax.ShapeDtypeStruct((tok_count, width - 2 * HEAD_DIM), kind),
        in_specs=[VMEM] * (4 + len(steps)),
        out_specs=VMEM,
        scratch_shapes=[
            pltpu.VMEM((keys, HEAD_DIM), jnp.bfloat16),
            pltpu.VMEM((keys, 2 * HEAD_DIM), jnp.bfloat16),
        ],
        compiler_params=pltpu.CompilerParams(vmem_limit_bytes=KERNEL_VMEM),
        name="attend_far",
    )(used, span, *state, *pages)


def join_kernel(*refs):
    count = len(refs) - 3
    part_refs, (out_ref, wide_ref, sems) = refs[:count], refs[count:]
    me = lax.axis_index("cp")
    width = part_refs[0].shape[1]
    copies = []
    for step, part_ref in enumerate(part_refs):
        source = part_ref
        if step:
            source = wide_ref.at[step - 1]
            source[...] = part_ref[...].astype(jnp.float32)
        place = pl.ds(pl.multiple_of((me ^ step) * width, width), width)
        copy = pltpu.make_async_copy(source, out_ref.at[0, :, place], sems.at[step])
        copy.start()
        copies.append(copy)
    for copy in copies:
        copy.wait()


def join(parts):
    tok_count, width = parts[0].shape
    count = len(parts)
    return pl.pallas_call(
        join_kernel,
        out_shape=jax.ShapeDtypeStruct((1, tok_count, count * width), jnp.float32),
        in_specs=[VMEM] * count,
        out_specs=ANY,
        scratch_shapes=[
            pltpu.VMEM((count - 1, tok_count, width), jnp.float32),
            pltpu.SemaphoreType.DMA((count,)),
        ],
        compiler_params=pltpu.CompilerParams(vmem_limit_bytes=SMALL),
        name="join",
    )(*parts)


def swap(x, axis, step):
    return lax.ppermute(x, axis, [(i, i ^ step) for i in range(lax.axis_size(axis))])


def body(queries, span_keys, span_values, pool_keys, pool_values, page_ids, prefix_pages):
    pool_count = lax.axis_size("pool")
    ctx_count = lax.axis_size("cp")
    packed, pages, used = pack(
        page_ids, prefix_pages, queries, span_keys, span_values, pool_keys, pool_values
    )
    span = lax.all_to_all(packed, "cp", split_axis=0, concat_axis=0, tiled=True)
    fetched = [swap(part, "pool", step) if step else part for step, part in enumerate(pages)]
    near = tuple(range(pool_count // 2))
    far = tuple(range(pool_count // 2, pool_count))
    state = attend_near(used, span, fetched[: len(near)], near)
    parts = [None] * ctx_count
    for step in reversed(range(ctx_count)):
        part = attend_far(used, span, state, fetched[len(near) :], far, step)
        parts[step] = swap(part, "cp", step) if step else part
    return join(parts)


def solution(mesh):
    in_specs = (
        P("pool", "cp", None),
        P("pool", "cp", None),
        P("pool", "cp", None),
        P("pool", None, None),
        P("pool", None, None),
        P(),
        P(),
    )
    out_specs = P("pool", "cp", None)
    return jax.shard_map(body, mesh=mesh, in_specs=in_specs, out_specs=out_specs, check_vma=False)
```

```python
import functools
import math

import jax
import jax.numpy as jnp
from jax import lax
from jax.experimental import pallas as pl
from jax.experimental.pallas import tpu as pltpu
from jax.sharding import PartitionSpec as P

HEAD_DIM = 128
HEADS = 32
KV_HEADS = 4
CAP = 2

NEG_FILL = -1e30
EXP2_SCALE = math.log2(math.e) / math.sqrt(HEAD_DIM)
SMALL = 8 * 2**20
KERNEL_VMEM = 32 * 2**20
ROWS = 128
ANY = pl.BlockSpec(memory_space=pl.ANY)
HBM = pl.BlockSpec(memory_space=pltpu.HBM)
SMEM = pl.BlockSpec(memory_space=pltpu.SMEM)
VMEM = pl.BlockSpec(memory_space=pltpu.VMEM)


def kv_head(ctx, ctx_count):
    return ctx * KV_HEADS // ctx_count


def pack_kernel(ids_hbm, len_hbm, q_ref, k_ref, v_ref, keys_ref, values_ref, *rest):
    span_out, rest = rest[0], rest[1:]
    pool_count, slot_count = ids_hbm.shape
    page_outs, rest = rest[:pool_count], rest[pool_count:]
    used_ref, ids_ref, len_ref, found_ref, span_ref, pages_ref, list_sems, span_sems, sems, out_sems = rest
    ctx_count = span_ref.shape[0]
    pages_dev = keys_ref.shape[0]
    me = lax.axis_index("pool")
    lists = [
        pltpu.make_async_copy(ids_hbm, ids_ref, list_sems.at[0]),
        pltpu.make_async_copy(len_hbm, len_ref, list_sems.at[1]),
    ]
    for copy in lists:
        copy.start()
    width = HEADS // ctx_count * HEAD_DIM
    span_copies = []
    for ctx in range(ctx_count):
        head = kv_head(ctx, ctx_count) * HEAD_DIM
        for part, (source, begin, size, place) in enumerate(
            (
                (q_ref, ctx * width, width, 0),
                (k_ref, head, HEAD_DIM, width),
                (v_ref, head, HEAD_DIM, width + HEAD_DIM),
            )
        ):
            copy = pltpu.make_async_copy(
                source.at[0, :, pl.ds(begin, size)],
                span_ref.at[ctx, :, pl.ds(place, size)],
                span_sems.at[ctx, part],
            )
            copy.start()
            span_copies.append(copy)
    for copy in lists:
        copy.wait()
    head = kv_head(lax.axis_index("cp"), ctx_count)
    columns = pl.ds(pl.multiple_of(head * HEAD_DIM, HEAD_DIM), HEAD_DIM)
    low = me * pages_dev
    page_copies = []
    for step in reversed(range(pool_count)):
        request = me ^ step
        live = len_ref[request]
        for rank in range(CAP):
            found_ref[step, rank] = 0
        count = jnp.int32(0)
        for slot in range(slot_count):
            local = ids_ref[request, slot] - low
            hit = (local >= 0) & (local < pages_dev) & (slot < live)
            found_ref[step, count] = jnp.where(hit, local, 0)
            count = jnp.minimum(count + hit.astype(jnp.int32), CAP)
        for rank in range(CAP):
            page = found_ref[step, rank]
            for which, source in enumerate((keys_ref, values_ref)):
                copy = pltpu.make_async_copy(
                    source.at[page, :, columns],
                    pages_ref.at[step, which, rank],
                    sems.at[step, which, rank],
                )
                copy.start()
                page_copies.append(copy)
    out_copies = [pltpu.make_async_copy(span_ref, span_out, out_sems.at[pool_count])]
    for copy in span_copies:
        copy.wait()
    out_copies[0].start()
    live = len_ref[me]
    for step in range(pool_count):
        count = jnp.int32(0)
        low = (me ^ step) * pages_dev
        for slot in range(slot_count):
            local = ids_ref[me, slot] - low
            hit = (local >= 0) & (local < pages_dev) & (slot < live)
            count = count + hit.astype(jnp.int32)
        for rank in range(CAP):
            row = step * CAP + rank
            used_ref[row : row + 1, :] = jnp.full(
                (1, HEAD_DIM), jnp.where(count > rank, 1.0, 0.0), jnp.float32
            )
    for index, step in enumerate(reversed(range(pool_count))):
        for copy in page_copies[index * 2 * CAP : (index + 1) * 2 * CAP]:
            copy.wait()
        copy = pltpu.make_async_copy(pages_ref.at[step], page_outs[step], out_sems.at[step])
        copy.start()
        out_copies.append(copy)
    for copy in out_copies:
        copy.wait()


def pack(page_ids, prefix_pages, queries, span_keys, span_values, pool_keys, pool_values):
    ctx_count = lax.axis_size("cp")
    tok_count = queries.shape[1]
    width = (HEADS // ctx_count + 2) * HEAD_DIM
    pool_count = page_ids.shape[0]
    page = pool_keys.shape[1]
    span_shape = (ctx_count, tok_count, width)
    page_shape = (2, CAP, page, HEAD_DIM)
    span, *pages, used = pl.pallas_call(
        pack_kernel,
        out_shape=[jax.ShapeDtypeStruct(span_shape, jnp.bfloat16)]
        + [jax.ShapeDtypeStruct(page_shape, jnp.bfloat16)] * pool_count
        + [jax.ShapeDtypeStruct((pool_count * CAP, HEAD_DIM), jnp.float32)],
        in_specs=[HBM] * 7,
        out_specs=[HBM] * (1 + pool_count) + [VMEM],
        scratch_shapes=[
            pltpu.SMEM(page_ids.shape, jnp.int32),
            pltpu.SMEM(prefix_pages.shape, jnp.int32),
            pltpu.SMEM((pool_count, CAP + 1), jnp.int32),
            pltpu.VMEM(span_shape, jnp.bfloat16),
            pltpu.VMEM((pool_count,) + page_shape, jnp.bfloat16),
            pltpu.SemaphoreType.DMA((2,)),
            pltpu.SemaphoreType.DMA((ctx_count, 3)),
            pltpu.SemaphoreType.DMA((pool_count, 2, CAP)),
            pltpu.SemaphoreType.DMA((pool_count + 1,)),
        ],
        compiler_params=pltpu.CompilerParams(vmem_limit_bytes=59 * 2**20),
        name="pack",
    )(page_ids, prefix_pages, queries, span_keys, span_values, pool_keys, pool_values)
    return span, pages, used


def place_pages(steps, used_ref, page_refs, k_ref, v_ref):
    page = page_refs[0].shape[2]
    ones = jnp.ones((page, HEAD_DIM), jnp.bfloat16)
    biases = []
    row = 0
    for step, page_ref in zip(steps, page_refs):
        for rank in range(CAP):
            rows = pl.ds(row, page)
            used = used_ref[step * CAP + rank : step * CAP + rank + 1, :]
            kept = jnp.broadcast_to(used, (page, HEAD_DIM)).astype(jnp.bfloat16)
            k_ref[rows, :] = page_ref[0, rank]
            v_ref[rows, :HEAD_DIM] = page_ref[1, rank] * kept
            v_ref[rows, HEAD_DIM:] = ones * kept
            biases.append((1.0 - used) * NEG_FILL)
            row += page
    return jnp.concatenate(biases, axis=1)


def stack_heads(span_ref, ctx, first, count):
    return jnp.concatenate(
        [
            span_ref[ctx, :, h * HEAD_DIM : (h + 1) * HEAD_DIM]
            for h in range(first, first + count)
        ],
        axis=0,
    )


def score(query, keys):
    return lax.dot_general(
        query, keys, (((1,), (1,)), ((), ())), preferred_element_type=jnp.float32
    )


def weigh(part, peak, values):
    weights = jnp.exp2((part - peak) * EXP2_SCALE).astype(jnp.bfloat16)
    return jnp.dot(weights, values, preferred_element_type=jnp.float32)


def near_kernel(steps, used_ref, span_ref, *rest):
    page_refs = rest[: len(steps)]
    sum_ref, peak_ref, k_ref, v_ref = rest[len(steps) :]
    ctx_count, tok_count, width = span_ref.shape
    heads = width // HEAD_DIM - 2
    bias = place_pages(steps, used_ref, page_refs, k_ref, v_ref)
    prefix = k_ref.shape[0] - ctx_count * tok_count
    for ctx in range(ctx_count):
        rows = pl.ds(prefix + ctx * tok_count, tok_count)
        k_ref[rows, :] = span_ref[ctx, :, heads * HEAD_DIM : (heads + 1) * HEAD_DIM]
        v_ref[rows, :HEAD_DIM] = span_ref[ctx, :, (heads + 1) * HEAD_DIM :]
        v_ref[rows, HEAD_DIM:] = jnp.ones((tok_count, HEAD_DIM), jnp.bfloat16)

    row_pos = lax.broadcasted_iota(jnp.int32, (tok_count, tok_count), 0)
    col_pos = lax.broadcasted_iota(jnp.int32, (tok_count, tok_count), 1)
    group = ROWS // tok_count
    causal = jnp.concatenate([col_pos <= row_pos] * group, axis=0)
    for ctx in range(ctx_count):
        begin = prefix + ctx * tok_count
        end = begin + tok_count
        for first in range(0, heads, group):
            rows = pl.ds(first * tok_count, group * tok_count)
            part = score(stack_heads(span_ref, ctx, first, group), k_ref[:end, :])
            pieces = [part[:, :prefix] + bias]
            if ctx:
                pieces.append(part[:, prefix:begin])
            pieces.append(jnp.where(causal, part[:, begin:], NEG_FILL))
            part = jnp.concatenate(pieces, axis=1)
            peak = jnp.max(part, axis=1, keepdims=True)
            sum_ref[ctx, rows, :] = weigh(part, peak, v_ref[:end, :])
            peak_ref[ctx, rows, :] = jnp.broadcast_to(peak, (group * tok_count, HEAD_DIM))


def attend_near(used, span, pages, steps):
    ctx_count, tok_count, width = span.shape
    page = pages[0].shape[2]
    keys = len(steps) * CAP * page + ctx_count * tok_count
    rows = (width // HEAD_DIM - 2) * tok_count
    return pl.pallas_call(
        functools.partial(near_kernel, steps),
        out_shape=[
            jax.ShapeDtypeStruct((ctx_count, rows, 2 * HEAD_DIM), jnp.float32),
            jax.ShapeDtypeStruct((ctx_count, rows, HEAD_DIM), jnp.float32),
        ],
        in_specs=[VMEM] * (2 + len(steps)),
        out_specs=[VMEM, VMEM],
        scratch_shapes=[
            pltpu.VMEM((keys, HEAD_DIM), jnp.bfloat16),
            pltpu.VMEM((keys, 2 * HEAD_DIM), jnp.bfloat16),
        ],
        compiler_params=pltpu.CompilerParams(vmem_limit_bytes=KERNEL_VMEM),
        name="attend_near",
    )(used, span, *pages)


def far_kernel(steps, ctx_steps, used_ref, span_ref, sum_ref, peak_ref, *rest):
    page_refs, rest = rest[: len(steps)], rest[len(steps) :]
    out_refs, (k_ref, v_ref) = rest[: len(ctx_steps)], rest[len(ctx_steps) :]
    tok_count = span_ref.shape[1]
    bias = place_pages(steps, used_ref, page_refs, k_ref, v_ref)
    group = ROWS // tok_count
    for ctx_step, out_ref in zip(ctx_steps, out_refs):
        ctx = lax.axis_index("cp") ^ ctx_step
        for first in range(0, span_ref.shape[2] // HEAD_DIM - 2, group):
            rows = pl.ds(first * tok_count, group * tok_count)
            part = score(stack_heads(span_ref, ctx, first, group), k_ref[...]) + bias
            near_peak = peak_ref[ctx, rows, :1]
            peak = jnp.maximum(jnp.max(part, axis=1, keepdims=True), near_peak)
            total = weigh(part, peak, v_ref[...])
            total = total + sum_ref[ctx, rows, :] * jnp.exp2((near_peak - peak) * EXP2_SCALE)
            mixed = (total[:, :HEAD_DIM] / total[:, HEAD_DIM:]).astype(out_ref.dtype)
            for h in range(group):
                place = (first + h) * HEAD_DIM
                out_ref[:, place : place + HEAD_DIM] = mixed[h * tok_count : (h + 1) * tok_count]


def attend_far(used, span, state, pages, steps, ctx_steps):
    ctx_count, tok_count, width = span.shape
    keys = len(steps) * CAP * pages[0].shape[2]
    kinds = [jnp.bfloat16 if step else jnp.float32 for step in ctx_steps]
    return pl.pallas_call(
        functools.partial(far_kernel, steps, ctx_steps),
        out_shape=[
            jax.ShapeDtypeStruct((tok_count, width - 2 * HEAD_DIM), kind) for kind in kinds
        ],
        in_specs=[VMEM] * (4 + len(steps)),
        out_specs=[VMEM] * len(ctx_steps),
        scratch_shapes=[
            pltpu.VMEM((keys, HEAD_DIM), jnp.bfloat16),
            pltpu.VMEM((keys, 2 * HEAD_DIM), jnp.bfloat16),
        ],
        compiler_params=pltpu.CompilerParams(vmem_limit_bytes=KERNEL_VMEM),
        name="attend_far",
    )(used, span, *state, *pages)


def join_kernel(*refs):
    count = len(refs) - 3
    part_refs, (out_ref, wide_ref, sems) = refs[:count], refs[count:]
    me = lax.axis_index("cp")
    width = part_refs[0].shape[1]
    copies = []
    for step, part_ref in enumerate(part_refs):
        source = part_ref
        if step:
            source = wide_ref.at[step - 1]
            source[...] = part_ref[...].astype(jnp.float32)
        place = pl.ds(pl.multiple_of((me ^ step) * width, width), width)
        copy = pltpu.make_async_copy(source, out_ref.at[0, :, place], sems.at[step])
        copy.start()
        copies.append(copy)
    for copy in copies:
        copy.wait()


def join(parts):
    tok_count, width = parts[0].shape
    count = len(parts)
    return pl.pallas_call(
        join_kernel,
        out_shape=jax.ShapeDtypeStruct((1, tok_count, count * width), jnp.float32),
        in_specs=[VMEM] * count,
        out_specs=ANY,
        scratch_shapes=[
            pltpu.VMEM((count - 1, tok_count, width), jnp.float32),
            pltpu.SemaphoreType.DMA((count,)),
        ],
        compiler_params=pltpu.CompilerParams(vmem_limit_bytes=SMALL),
        name="join",
    )(*parts)


def swap(x, axis, step):
    return lax.ppermute(x, axis, [(i, i ^ step) for i in range(lax.axis_size(axis))])


def body(queries, span_keys, span_values, pool_keys, pool_values, page_ids, prefix_pages):
    pool_count = lax.axis_size("pool")
    ctx_count = lax.axis_size("cp")
    packed, pages, used = pack(
        page_ids, prefix_pages, queries, span_keys, span_values, pool_keys, pool_values
    )
    span = lax.all_to_all(packed, "cp", split_axis=0, concat_axis=0, tiled=True)
    fetched = [swap(part, "pool", step) if step else part for step, part in enumerate(pages)]
    near = tuple(step for step in range(pool_count) if step % 4 < 2)
    far = tuple(step for step in range(pool_count) if step % 4 >= 2)
    state = attend_near(used, span, [fetched[step] for step in near], near)
    parts = [None] * ctx_count
    order = ((ctx_count - 1,), tuple(range(1, ctx_count - 1)), (0,))
    for ctx_steps in order:
        out = attend_far(used, span, state, [fetched[step] for step in far], far, ctx_steps)
        for step, part in zip(ctx_steps, out):
            parts[step] = swap(part, "cp", step) if step else part
    return join(parts)


def solution(mesh):
    in_specs = (
        P("pool", "cp", None),
        P("pool", "cp", None),
        P("pool", "cp", None),
        P("pool", None, None),
        P("pool", None, None),
        P(),
        P(),
    )
    out_specs = P("pool", "cp", None)
    return jax.shard_map(body, mesh=mesh, in_specs=in_specs, out_specs=out_specs, check_vma=False)
```

```python
import functools
import math

import jax
import jax.numpy as jnp
from jax import lax
from jax.experimental import pallas as pl
from jax.experimental.pallas import tpu as pltpu
from jax.sharding import PartitionSpec as P

HEAD_DIM = 128
HEADS = 32
KV_HEADS = 4
CAP = 2

NEG_FILL = -1e30
EXP2_SCALE = math.log2(math.e) / math.sqrt(HEAD_DIM)
SMALL = 8 * 2**20
KERNEL_VMEM = 32 * 2**20
ROWS = 128
ANY = pl.BlockSpec(memory_space=pl.ANY)
HBM = pl.BlockSpec(memory_space=pltpu.HBM)
SMEM = pl.BlockSpec(memory_space=pltpu.SMEM)
VMEM = pl.BlockSpec(memory_space=pltpu.VMEM)


def kv_head(ctx, ctx_count):
    return ctx * KV_HEADS // ctx_count


def pack_kernel(ids_hbm, len_hbm, q_ref, k_ref, v_ref, keys_ref, values_ref, *rest):
    span_out, rest = rest[0], rest[1:]
    pool_count, slot_count = ids_hbm.shape
    page_outs, rest = rest[:pool_count], rest[pool_count:]
    used_ref, ids_ref, len_ref, found_ref, span_ref, pages_ref, list_sems, span_sems, sems, out_sems = rest
    ctx_count = span_ref.shape[0]
    pages_dev = keys_ref.shape[0]
    me = lax.axis_index("pool")
    lists = [
        pltpu.make_async_copy(ids_hbm, ids_ref, list_sems.at[0]),
        pltpu.make_async_copy(len_hbm, len_ref, list_sems.at[1]),
    ]
    for copy in lists:
        copy.start()
    width = HEADS // ctx_count * HEAD_DIM
    span_copies = []
    for ctx in range(ctx_count):
        head = kv_head(ctx, ctx_count) * HEAD_DIM
        for part, (source, begin, size, place) in enumerate(
            (
                (q_ref, ctx * width, width, 0),
                (k_ref, head, HEAD_DIM, width),
                (v_ref, head, HEAD_DIM, width + HEAD_DIM),
            )
        ):
            copy = pltpu.make_async_copy(
                source.at[0, :, pl.ds(begin, size)],
                span_ref.at[ctx, :, pl.ds(place, size)],
                span_sems.at[ctx, part],
            )
            copy.start()
            span_copies.append(copy)
    for copy in lists:
        copy.wait()
    head = kv_head(lax.axis_index("cp"), ctx_count)
    columns = pl.ds(pl.multiple_of(head * HEAD_DIM, HEAD_DIM), HEAD_DIM)
    low = me * pages_dev
    page_copies = []
    for step in reversed(range(pool_count)):
        request = me ^ step
        live = len_ref[request]
        for rank in range(CAP):
            found_ref[step, rank] = 0
        count = jnp.int32(0)
        for slot in range(slot_count):
            local = ids_ref[request, slot] - low
            hit = (local >= 0) & (local < pages_dev) & (slot < live)
            found_ref[step, count] = jnp.where(hit, local, 0)
            count = jnp.minimum(count + hit.astype(jnp.int32), CAP)
        for rank in range(CAP):
            page = found_ref[step, rank]
            for which, source in enumerate((keys_ref, values_ref)):
                copy = pltpu.make_async_copy(
                    source.at[page, :, columns],
                    pages_ref.at[step, which, rank],
                    sems.at[step, which, rank],
                )
                copy.start()
                page_copies.append(copy)
    out_copies = [pltpu.make_async_copy(span_ref, span_out, out_sems.at[pool_count])]
    for copy in span_copies:
        copy.wait()
    out_copies[0].start()
    live = len_ref[me]
    for step in range(pool_count):
        count = jnp.int32(0)
        low = (me ^ step) * pages_dev
        for slot in range(slot_count):
            local = ids_ref[me, slot] - low
            hit = (local >= 0) & (local < pages_dev) & (slot < live)
            count = count + hit.astype(jnp.int32)
        for rank in range(CAP):
            row = step * CAP + rank
            used_ref[row : row + 1, :] = jnp.full(
                (1, HEAD_DIM), jnp.where(count > rank, 1.0, 0.0), jnp.float32
            )
    for index, step in enumerate(reversed(range(pool_count))):
        for copy in page_copies[index * 2 * CAP : (index + 1) * 2 * CAP]:
            copy.wait()
        copy = pltpu.make_async_copy(pages_ref.at[step], page_outs[step], out_sems.at[step])
        copy.start()
        out_copies.append(copy)
    for copy in out_copies:
        copy.wait()


def pack(page_ids, prefix_pages, queries, span_keys, span_values, pool_keys, pool_values):
    ctx_count = lax.axis_size("cp")
    tok_count = queries.shape[1]
    width = (HEADS // ctx_count + 2) * HEAD_DIM
    pool_count = page_ids.shape[0]
    page = pool_keys.shape[1]
    span_shape = (ctx_count, tok_count, width)
    page_shape = (2, CAP, page, HEAD_DIM)
    span, *pages, used = pl.pallas_call(
        pack_kernel,
        out_shape=[jax.ShapeDtypeStruct(span_shape, jnp.bfloat16)]
        + [jax.ShapeDtypeStruct(page_shape, jnp.bfloat16)] * pool_count
        + [jax.ShapeDtypeStruct((pool_count * CAP, HEAD_DIM), jnp.float32)],
        in_specs=[HBM] * 7,
        out_specs=[HBM] * (1 + pool_count) + [VMEM],
        scratch_shapes=[
            pltpu.SMEM(page_ids.shape, jnp.int32),
            pltpu.SMEM(prefix_pages.shape, jnp.int32),
            pltpu.SMEM((pool_count, CAP + 1), jnp.int32),
            pltpu.VMEM(span_shape, jnp.bfloat16),
            pltpu.VMEM((pool_count,) + page_shape, jnp.bfloat16),
            pltpu.SemaphoreType.DMA((2,)),
            pltpu.SemaphoreType.DMA((ctx_count, 3)),
            pltpu.SemaphoreType.DMA((pool_count, 2, CAP)),
            pltpu.SemaphoreType.DMA((pool_count + 1,)),
        ],
        compiler_params=pltpu.CompilerParams(vmem_limit_bytes=59 * 2**20),
        name="pack",
    )(page_ids, prefix_pages, queries, span_keys, span_values, pool_keys, pool_values)
    return span, pages, used


def place_pages(steps, used_ref, page_refs, k_ref, v_ref):
    page = page_refs[0].shape[2]
    ones = jnp.ones((page, HEAD_DIM), jnp.bfloat16)
    biases = []
    row = 0
    for step, page_ref in zip(steps, page_refs):
        for rank in range(CAP):
            rows = pl.ds(row, page)
            used = used_ref[step * CAP + rank : step * CAP + rank + 1, :]
            kept = jnp.broadcast_to(used, (page, HEAD_DIM)).astype(jnp.bfloat16)
            k_ref[rows, :] = page_ref[0, rank]
            v_ref[rows, :HEAD_DIM] = page_ref[1, rank] * kept
            v_ref[rows, HEAD_DIM:] = ones * kept
            biases.append((1.0 - used) * NEG_FILL)
            row += page
    return jnp.concatenate(biases, axis=1)


def stack_heads(span_ref, ctx, first, count):
    return jnp.concatenate(
        [
            span_ref[ctx, :, h * HEAD_DIM : (h + 1) * HEAD_DIM]
            for h in range(first, first + count)
        ],
        axis=0,
    )


def score(query, keys):
    return lax.dot_general(
        query, keys, (((1,), (1,)), ((), ())), preferred_element_type=jnp.float32
    )


def weigh(part, peak, values):
    weights = jnp.exp2((part - peak) * EXP2_SCALE).astype(jnp.bfloat16)
    return jnp.dot(weights, values, preferred_element_type=jnp.float32)


def near_kernel(steps, used_ref, span_ref, *rest):
    page_refs = rest[: len(steps)]
    sum_ref, peak_ref, k_ref, v_ref = rest[len(steps) :]
    ctx_count, tok_count, width = span_ref.shape
    heads = width // HEAD_DIM - 2
    bias = place_pages(steps, used_ref, page_refs, k_ref, v_ref)
    prefix = k_ref.shape[0] - ctx_count * tok_count
    for ctx in range(ctx_count):
        rows = pl.ds(prefix + ctx * tok_count, tok_count)
        k_ref[rows, :] = span_ref[ctx, :, heads * HEAD_DIM : (heads + 1) * HEAD_DIM]
        v_ref[rows, :HEAD_DIM] = span_ref[ctx, :, (heads + 1) * HEAD_DIM :]
        v_ref[rows, HEAD_DIM:] = jnp.ones((tok_count, HEAD_DIM), jnp.bfloat16)

    row_pos = lax.broadcasted_iota(jnp.int32, (tok_count, tok_count), 0)
    col_pos = lax.broadcasted_iota(jnp.int32, (tok_count, tok_count), 1)
    group = ROWS // tok_count
    causal = jnp.concatenate([col_pos <= row_pos] * group, axis=0)
    for ctx in range(ctx_count):
        begin = prefix + ctx * tok_count
        end = begin + tok_count
        for first in range(0, heads, group):
            rows = pl.ds(first * tok_count, group * tok_count)
            part = score(stack_heads(span_ref, ctx, first, group), k_ref[:end, :])
            pieces = [part[:, :prefix] + bias]
            if ctx:
                pieces.append(part[:, prefix:begin])
            pieces.append(jnp.where(causal, part[:, begin:], NEG_FILL))
            part = jnp.concatenate(pieces, axis=1)
            peak = jnp.max(part, axis=1, keepdims=True)
            sum_ref[ctx, rows, :] = weigh(part, peak, v_ref[:end, :])
            peak_ref[ctx, rows, :] = jnp.broadcast_to(peak, (group * tok_count, HEAD_DIM))


def attend_near(used, span, pages, steps):
    ctx_count, tok_count, width = span.shape
    page = pages[0].shape[2]
    keys = len(steps) * CAP * page + ctx_count * tok_count
    rows = (width // HEAD_DIM - 2) * tok_count
    return pl.pallas_call(
        functools.partial(near_kernel, steps),
        out_shape=[
            jax.ShapeDtypeStruct((ctx_count, rows, 2 * HEAD_DIM), jnp.float32),
            jax.ShapeDtypeStruct((ctx_count, rows, HEAD_DIM), jnp.float32),
        ],
        in_specs=[VMEM] * (2 + len(steps)),
        out_specs=[VMEM, VMEM],
        scratch_shapes=[
            pltpu.VMEM((keys, HEAD_DIM), jnp.bfloat16),
            pltpu.VMEM((keys, 2 * HEAD_DIM), jnp.bfloat16),
        ],
        compiler_params=pltpu.CompilerParams(vmem_limit_bytes=KERNEL_VMEM),
        name="attend_near",
    )(used, span, *pages)


def far_kernel(steps, ctx_steps, used_ref, span_ref, sum_ref, peak_ref, *rest):
    page_refs, rest = rest[: len(steps)], rest[len(steps) :]
    out_refs, (k_ref, v_ref) = rest[: len(ctx_steps)], rest[len(ctx_steps) :]
    tok_count = span_ref.shape[1]
    bias = place_pages(steps, used_ref, page_refs, k_ref, v_ref)
    group = ROWS // tok_count
    for ctx_step, out_ref in zip(ctx_steps, out_refs):
        ctx = lax.axis_index("cp") ^ ctx_step
        for first in range(0, span_ref.shape[2] // HEAD_DIM - 2, group):
            rows = pl.ds(first * tok_count, group * tok_count)
            part = score(stack_heads(span_ref, ctx, first, group), k_ref[...]) + bias
            near_peak = peak_ref[ctx, rows, :1]
            peak = jnp.maximum(jnp.max(part, axis=1, keepdims=True), near_peak)
            total = weigh(part, peak, v_ref[...])
            total = total + sum_ref[ctx, rows, :] * jnp.exp2((near_peak - peak) * EXP2_SCALE)
            mixed = (total[:, :HEAD_DIM] / total[:, HEAD_DIM:]).astype(out_ref.dtype)
            for h in range(group):
                place = (first + h) * HEAD_DIM
                out_ref[:, place : place + HEAD_DIM] = mixed[h * tok_count : (h + 1) * tok_count]


def attend_far(used, span, state, pages, steps, ctx_steps):
    ctx_count, tok_count, width = span.shape
    keys = len(steps) * CAP * pages[0].shape[2]
    kinds = [jnp.bfloat16 if step else jnp.float32 for step in ctx_steps]
    return pl.pallas_call(
        functools.partial(far_kernel, steps, ctx_steps),
        out_shape=[
            jax.ShapeDtypeStruct((tok_count, width - 2 * HEAD_DIM), kind) for kind in kinds
        ],
        in_specs=[VMEM] * (4 + len(steps)),
        out_specs=[VMEM] * len(ctx_steps),
        scratch_shapes=[
            pltpu.VMEM((keys, HEAD_DIM), jnp.bfloat16),
            pltpu.VMEM((keys, 2 * HEAD_DIM), jnp.bfloat16),
        ],
        compiler_params=pltpu.CompilerParams(vmem_limit_bytes=KERNEL_VMEM),
        name="attend_far",
    )(used, span, *state, *pages)


def join_kernel(steps, *refs):
    part_refs, (out_ref, wide_ref, sems) = refs[: len(steps)], refs[-3:]
    me = lax.axis_index("cp")
    width = part_refs[0].shape[1]
    copies = []
    for index, (step, part_ref) in enumerate(zip(steps, part_refs)):
        source = wide_ref.at[index]
        source[...] = part_ref[...].astype(jnp.float32)
        place = pl.ds(pl.multiple_of((me ^ step) * width, width), width)
        copy = pltpu.make_async_copy(source, out_ref.at[0, :, place], sems.at[index])
        copy.start()
        copies.append(copy)
    for copy in copies:
        copy.wait()


def join(parts, steps, count, into=None):
    tok_count, width = parts[0].shape
    return pl.pallas_call(
        functools.partial(join_kernel, steps),
        out_shape=jax.ShapeDtypeStruct((1, tok_count, count * width), jnp.float32),
        in_specs=[VMEM] * len(steps) + ([] if into is None else [HBM]),
        out_specs=HBM,
        scratch_shapes=[
            pltpu.VMEM((len(steps), tok_count, width), jnp.float32),
            pltpu.SemaphoreType.DMA((len(steps),)),
        ],
        input_output_aliases={} if into is None else {len(steps): 0},
        compiler_params=pltpu.CompilerParams(vmem_limit_bytes=SMALL),
        name="join",
    )(*parts, *([] if into is None else [into]))


def swap(x, axis, step):
    return lax.ppermute(x, axis, [(i, i ^ step) for i in range(lax.axis_size(axis))])


def body(queries, span_keys, span_values, pool_keys, pool_values, page_ids, prefix_pages):
    pool_count = lax.axis_size("pool")
    ctx_count = lax.axis_size("cp")
    packed, pages, used = pack(
        page_ids, prefix_pages, queries, span_keys, span_values, pool_keys, pool_values
    )
    span = lax.all_to_all(packed, "cp", split_axis=0, concat_axis=0, tiled=True)
    fetched = [swap(part, "pool", step) if step else part for step, part in enumerate(pages)]
    near = tuple(step for step in range(pool_count) if step % 4 < 2)
    far = tuple(step for step in range(pool_count) if step % 4 >= 2)
    state = attend_near(used, span, [fetched[step] for step in near], near)
    parts = [None] * ctx_count
    order = ((ctx_count - 1,), tuple(range(1, ctx_count - 1)), (0,))
    for ctx_steps in order:
        out = attend_far(used, span, state, [fetched[step] for step in far], far, ctx_steps)
        for step, part in zip(ctx_steps, out):
            parts[step] = swap(part, "cp", step) if step else part
    early, late = (0, ctx_count - 1), tuple(range(1, ctx_count - 1))
    attended = join([parts[step] for step in early], early, ctx_count)
    return join([parts[step] for step in late], late, ctx_count, attended)


def solution(mesh):
    in_specs = (
        P("pool", "cp", None),
        P("pool", "cp", None),
        P("pool", "cp", None),
        P("pool", None, None),
        P("pool", None, None),
        P(),
        P(),
    )
    out_specs = P("pool", "cp", None)
    return jax.shard_map(body, mesh=mesh, in_specs=in_specs, out_specs=out_specs, check_vma=False)
```

```python
import functools
import math

import jax
import jax.numpy as jnp
from jax import lax
from jax.experimental import pallas as pl
from jax.experimental.pallas import tpu as pltpu
from jax.sharding import PartitionSpec as P

HEAD_DIM = 128
HEADS = 32
KV_HEADS = 4
CAP = 2

NEG_FILL = -1e30
EXP2_SCALE = math.log2(math.e) / math.sqrt(HEAD_DIM)
SMALL = 8 * 2**20
KERNEL_VMEM = 32 * 2**20
ROWS = 128
ANY = pl.BlockSpec(memory_space=pl.ANY)
HBM = pl.BlockSpec(memory_space=pltpu.HBM)
SMEM = pl.BlockSpec(memory_space=pltpu.SMEM)
VMEM = pl.BlockSpec(memory_space=pltpu.VMEM)


def kv_head(ctx, ctx_count):
    return ctx * KV_HEADS // ctx_count


def pack_kernel(ids_hbm, len_hbm, q_ref, k_ref, v_ref, keys_ref, values_ref, *rest):
    span_out, rest = rest[0], rest[1:]
    pool_count, slot_count = ids_hbm.shape
    page_outs, rest = rest[:pool_count], rest[pool_count:]
    used_ref, ids_ref, len_ref, span_ref, pages_ref, list_sems, span_sems, sems, out_sems = rest
    ctx_count = span_ref.shape[0]
    pages_dev = keys_ref.shape[0]
    me = lax.axis_index("pool")
    lists = [
        pltpu.make_async_copy(ids_hbm, ids_ref, list_sems.at[0]),
        pltpu.make_async_copy(len_hbm, len_ref, list_sems.at[1]),
    ]
    for copy in lists:
        copy.start()
    width = HEADS // ctx_count * HEAD_DIM
    span_copies = []
    for ctx in range(ctx_count):
        head = kv_head(ctx, ctx_count) * HEAD_DIM
        for part, (source, begin, size, place) in enumerate(
            (
                (q_ref, ctx * width, width, 0),
                (k_ref, head, HEAD_DIM, width),
                (v_ref, head, HEAD_DIM, width + HEAD_DIM),
            )
        ):
            copy = pltpu.make_async_copy(
                source.at[0, :, pl.ds(begin, size)],
                span_ref.at[ctx, :, pl.ds(place, size)],
                span_sems.at[ctx, part],
            )
            copy.start()
            span_copies.append(copy)
    for copy in lists:
        copy.wait()
    head = kv_head(lax.axis_index("cp"), ctx_count)
    columns = pl.ds(pl.multiple_of(head * HEAD_DIM, HEAD_DIM), HEAD_DIM)
    low = me * pages_dev
    page_copies = []
    for step in reversed(range(pool_count)):
        request = me ^ step
        live = len_ref[request]
        found = [jnp.int32(0)] * CAP
        count = jnp.int32(0)
        for slot in range(slot_count):
            local = ids_ref[request, slot] - low
            hit = (local >= 0) & (local < pages_dev) & (slot < live)
            found = [
                jnp.where(hit & (count == rank), local, page) for rank, page in enumerate(found)
            ]
            count = count + hit.astype(jnp.int32)
        for rank, page in enumerate(found):
            for which, source in enumerate((keys_ref, values_ref)):
                copy = pltpu.make_async_copy(
                    source.at[page, :, columns],
                    pages_ref.at[step, which, rank],
                    sems.at[step, which, rank],
                )
                copy.start()
                page_copies.append(copy)
    out_copies = [pltpu.make_async_copy(span_ref, span_out, out_sems.at[pool_count])]
    for copy in span_copies:
        copy.wait()
    out_copies[0].start()
    live = len_ref[me]
    for step in range(pool_count):
        count = jnp.int32(0)
        low = (me ^ step) * pages_dev
        for slot in range(slot_count):
            local = ids_ref[me, slot] - low
            hit = (local >= 0) & (local < pages_dev) & (slot < live)
            count = count + hit.astype(jnp.int32)
        for rank in range(CAP):
            row = step * CAP + rank
            used_ref[row : row + 1, :] = jnp.full(
                (1, HEAD_DIM), jnp.where(count > rank, 1.0, 0.0), jnp.float32
            )
    for index, step in enumerate(reversed(range(pool_count))):
        for copy in page_copies[index * 2 * CAP : (index + 1) * 2 * CAP]:
            copy.wait()
        copy = pltpu.make_async_copy(pages_ref.at[step], page_outs[step], out_sems.at[step])
        copy.start()
        out_copies.append(copy)
    for copy in out_copies:
        copy.wait()


def pack(page_ids, prefix_pages, queries, span_keys, span_values, pool_keys, pool_values):
    ctx_count = lax.axis_size("cp")
    tok_count = queries.shape[1]
    width = (HEADS // ctx_count + 2) * HEAD_DIM
    pool_count = page_ids.shape[0]
    page = pool_keys.shape[1]
    span_shape = (ctx_count, tok_count, width)
    page_shape = (2, CAP, page, HEAD_DIM)
    span, *pages, used = pl.pallas_call(
        pack_kernel,
        out_shape=[jax.ShapeDtypeStruct(span_shape, jnp.bfloat16)]
        + [jax.ShapeDtypeStruct(page_shape, jnp.bfloat16)] * pool_count
        + [jax.ShapeDtypeStruct((pool_count * CAP, HEAD_DIM), jnp.float32)],
        in_specs=[HBM] * 7,
        out_specs=[HBM] * (1 + pool_count) + [VMEM],
        scratch_shapes=[
            pltpu.SMEM(page_ids.shape, jnp.int32),
            pltpu.SMEM(prefix_pages.shape, jnp.int32),
            pltpu.VMEM(span_shape, jnp.bfloat16),
            pltpu.VMEM((pool_count,) + page_shape, jnp.bfloat16),
            pltpu.SemaphoreType.DMA((2,)),
            pltpu.SemaphoreType.DMA((ctx_count, 3)),
            pltpu.SemaphoreType.DMA((pool_count, 2, CAP)),
            pltpu.SemaphoreType.DMA((pool_count + 1,)),
        ],
        compiler_params=pltpu.CompilerParams(vmem_limit_bytes=59 * 2**20),
        name="pack",
    )(page_ids, prefix_pages, queries, span_keys, span_values, pool_keys, pool_values)
    return span, pages, used


def place_pages(steps, used_ref, page_refs, k_ref, v_ref):
    page = page_refs[0].shape[2]
    ones = jnp.ones((page, HEAD_DIM), jnp.bfloat16)
    biases = []
    row = 0
    for step, page_ref in zip(steps, page_refs):
        for rank in range(CAP):
            rows = pl.ds(row, page)
            used = used_ref[step * CAP + rank : step * CAP + rank + 1, :]
            kept = jnp.broadcast_to(used, (page, HEAD_DIM)).astype(jnp.bfloat16)
            k_ref[rows, :] = page_ref[0, rank]
            v_ref[rows, :HEAD_DIM] = page_ref[1, rank] * kept
            v_ref[rows, HEAD_DIM:] = ones * kept
            biases.append((1.0 - used) * NEG_FILL)
            row += page
    return jnp.concatenate(biases, axis=1)


def stack_heads(span_ref, ctx, first, count):
    return jnp.concatenate(
        [
            span_ref[ctx, :, h * HEAD_DIM : (h + 1) * HEAD_DIM]
            for h in range(first, first + count)
        ],
        axis=0,
    )


def score(query, keys):
    return lax.dot_general(
        query, keys, (((1,), (1,)), ((), ())), preferred_element_type=jnp.float32
    )


def weigh(part, peak, values):
    weights = jnp.exp2((part - peak) * EXP2_SCALE).astype(jnp.bfloat16)
    return jnp.dot(weights, values, preferred_element_type=jnp.float32)


def near_kernel(steps, used_ref, span_ref, *rest):
    page_refs = rest[: len(steps)]
    sum_ref, peak_ref, k_ref, v_ref = rest[len(steps) :]
    ctx_count, tok_count, width = span_ref.shape
    heads = width // HEAD_DIM - 2
    bias = place_pages(steps, used_ref, page_refs, k_ref, v_ref)
    prefix = k_ref.shape[0] - ctx_count * tok_count
    for ctx in range(ctx_count):
        rows = pl.ds(prefix + ctx * tok_count, tok_count)
        k_ref[rows, :] = span_ref[ctx, :, heads * HEAD_DIM : (heads + 1) * HEAD_DIM]
        v_ref[rows, :HEAD_DIM] = span_ref[ctx, :, (heads + 1) * HEAD_DIM :]
        v_ref[rows, HEAD_DIM:] = jnp.ones((tok_count, HEAD_DIM), jnp.bfloat16)

    row_pos = lax.broadcasted_iota(jnp.int32, (tok_count, tok_count), 0)
    col_pos = lax.broadcasted_iota(jnp.int32, (tok_count, tok_count), 1)
    group = ROWS // tok_count
    causal = jnp.concatenate([col_pos <= row_pos] * group, axis=0)
    for ctx in range(ctx_count):
        begin = prefix + ctx * tok_count
        end = begin + tok_count
        for first in range(0, heads, group):
            rows = pl.ds(first * tok_count, group * tok_count)
            part = score(stack_heads(span_ref, ctx, first, group), k_ref[:end, :])
            pieces = [part[:, :prefix] + bias]
            if ctx:
                pieces.append(part[:, prefix:begin])
            pieces.append(jnp.where(causal, part[:, begin:], NEG_FILL))
            part = jnp.concatenate(pieces, axis=1)
            peak = jnp.max(part, axis=1, keepdims=True)
            sum_ref[ctx, rows, :] = weigh(part, peak, v_ref[:end, :])
            peak_ref[ctx, rows, :] = jnp.broadcast_to(peak, (group * tok_count, HEAD_DIM))


def attend_near(used, span, pages, steps):
    ctx_count, tok_count, width = span.shape
    page = pages[0].shape[2]
    keys = len(steps) * CAP * page + ctx_count * tok_count
    rows = (width // HEAD_DIM - 2) * tok_count
    return pl.pallas_call(
        functools.partial(near_kernel, steps),
        out_shape=[
            jax.ShapeDtypeStruct((ctx_count, rows, 2 * HEAD_DIM), jnp.float32),
            jax.ShapeDtypeStruct((ctx_count, rows, HEAD_DIM), jnp.float32),
        ],
        in_specs=[VMEM] * (2 + len(steps)),
        out_specs=[VMEM, VMEM],
        scratch_shapes=[
            pltpu.VMEM((keys, HEAD_DIM), jnp.bfloat16),
            pltpu.VMEM((keys, 2 * HEAD_DIM), jnp.bfloat16),
        ],
        compiler_params=pltpu.CompilerParams(vmem_limit_bytes=KERNEL_VMEM),
        name="attend_near",
    )(used, span, *pages)


def far_kernel(steps, ctx_steps, used_ref, span_ref, sum_ref, peak_ref, *rest):
    page_refs, rest = rest[: len(steps)], rest[len(steps) :]
    out_refs, (k_ref, v_ref) = rest[: len(ctx_steps)], rest[len(ctx_steps) :]
    tok_count = span_ref.shape[1]
    bias = place_pages(steps, used_ref, page_refs, k_ref, v_ref)
    group = ROWS // tok_count
    for ctx_step, out_ref in zip(ctx_steps, out_refs):
        ctx = lax.axis_index("cp") ^ ctx_step
        for first in range(0, span_ref.shape[2] // HEAD_DIM - 2, group):
            rows = pl.ds(first * tok_count, group * tok_count)
            part = score(stack_heads(span_ref, ctx, first, group), k_ref[...]) + bias
            near_peak = peak_ref[ctx, rows, :1]
            peak = jnp.maximum(jnp.max(part, axis=1, keepdims=True), near_peak)
            total = weigh(part, peak, v_ref[...])
            total = total + sum_ref[ctx, rows, :] * jnp.exp2((near_peak - peak) * EXP2_SCALE)
            mixed = (total[:, :HEAD_DIM] / total[:, HEAD_DIM:]).astype(out_ref.dtype)
            for h in range(group):
                place = (first + h) * HEAD_DIM
                out_ref[:, place : place + HEAD_DIM] = mixed[h * tok_count : (h + 1) * tok_count]


def attend_far(used, span, state, pages, steps, ctx_steps):
    ctx_count, tok_count, width = span.shape
    keys = len(steps) * CAP * pages[0].shape[2]
    kinds = [jnp.bfloat16 if step else jnp.float32 for step in ctx_steps]
    return pl.pallas_call(
        functools.partial(far_kernel, steps, ctx_steps),
        out_shape=[
            jax.ShapeDtypeStruct((tok_count, width - 2 * HEAD_DIM), kind) for kind in kinds
        ],
        in_specs=[VMEM] * (4 + len(steps)),
        out_specs=[VMEM] * len(ctx_steps),
        scratch_shapes=[
            pltpu.VMEM((keys, HEAD_DIM), jnp.bfloat16),
            pltpu.VMEM((keys, 2 * HEAD_DIM), jnp.bfloat16),
        ],
        compiler_params=pltpu.CompilerParams(vmem_limit_bytes=KERNEL_VMEM),
        name="attend_far",
    )(used, span, *state, *pages)


def join_kernel(steps, *refs):
    part_refs, (out_ref, wide_ref, sems) = refs[: len(steps)], refs[-3:]
    me = lax.axis_index("cp")
    width = part_refs[0].shape[1]
    copies = []
    for index, (step, part_ref) in enumerate(zip(steps, part_refs)):
        source = wide_ref.at[index]
        source[...] = part_ref[...].astype(jnp.float32)
        place = pl.ds(pl.multiple_of((me ^ step) * width, width), width)
        copy = pltpu.make_async_copy(source, out_ref.at[0, :, place], sems.at[index])
        copy.start()
        copies.append(copy)
    for copy in copies:
        copy.wait()


def join(parts, steps, count, into=None):
    tok_count, width = parts[0].shape
    return pl.pallas_call(
        functools.partial(join_kernel, steps),
        out_shape=jax.ShapeDtypeStruct((1, tok_count, count * width), jnp.float32),
        in_specs=[VMEM] * len(steps) + ([] if into is None else [HBM]),
        out_specs=HBM,
        scratch_shapes=[
            pltpu.VMEM((len(steps), tok_count, width), jnp.float32),
            pltpu.SemaphoreType.DMA((len(steps),)),
        ],
        input_output_aliases={} if into is None else {len(steps): 0},
        compiler_params=pltpu.CompilerParams(vmem_limit_bytes=SMALL),
        name="join",
    )(*parts, *([] if into is None else [into]))


def swap(x, axis, step):
    return lax.ppermute(x, axis, [(i, i ^ step) for i in range(lax.axis_size(axis))])


def body(queries, span_keys, span_values, pool_keys, pool_values, page_ids, prefix_pages):
    pool_count = lax.axis_size("pool")
    ctx_count = lax.axis_size("cp")
    packed, pages, used = pack(
        page_ids, prefix_pages, queries, span_keys, span_values, pool_keys, pool_values
    )
    span = lax.all_to_all(packed, "cp", split_axis=0, concat_axis=0, tiled=True)
    fetched = [swap(part, "pool", step) if step else part for step, part in enumerate(pages)]
    near = tuple(step for step in range(pool_count) if step % 4 < 2)
    far = tuple(step for step in range(pool_count) if step % 4 >= 2)
    state = attend_near(used, span, [fetched[step] for step in near], near)
    parts = [None] * ctx_count
    order = ((ctx_count - 1,), tuple(range(1, ctx_count - 1)), (0,))
    for ctx_steps in order:
        out = attend_far(used, span, state, [fetched[step] for step in far], far, ctx_steps)
        for step, part in zip(ctx_steps, out):
            parts[step] = swap(part, "cp", step) if step else part
    early, late = (0, ctx_count - 1), tuple(range(1, ctx_count - 1))
    attended = join([parts[step] for step in early], early, ctx_count)
    return join([parts[step] for step in late], late, ctx_count, attended)


def solution(mesh):
    in_specs = (
        P("pool", "cp", None),
        P("pool", "cp", None),
        P("pool", "cp", None),
        P("pool", None, None),
        P("pool", None, None),
        P(),
        P(),
    )
    out_specs = P("pool", "cp", None)
    return jax.shard_map(body, mesh=mesh, in_specs=in_specs, out_specs=out_specs, check_vma=False)
```
